32 devices in a mesh: dp: 2 (over x), depth: 4 (over y, core), height: 4 (over z).
Axes of the slice: x: 2, y: 2, z: 4, core: 2. Of those that a mesh axis runs over, the one named last changes fastest.
Arguments:
- volume: bfloat16 [2, 8, 32, 4096], P('dp', 'depth', 'height'), may hold values from -6 to 6
- feature_grad: bfloat16 [2, 8, 32, 4096], P('dp', 'depth', 'height'), may hold values from -0.125 to 0.125
- master_weights: float32 [2, 110592], P(None, ('dp', 'depth', 'height')), may hold values from -0.15625 to 0.15625
- first_moment: float32 [2, 110592], P(None, ('dp', 'depth', 'height')), may hold values from -3 to 3
- second_moment: float32 [2, 110592], P(None, ('dp', 'depth', 'height')), may hold values from 0.1 to 4
Outputs:
- features: bfloat16 [2, 8, 32, 4096], P('dp', 'depth', 'height')
- new_weights: float32 [2, 110592], P(None, ('dp', 'depth', 'height'))
- new_first: float32 [2, 110592], P(None, ('dp', 'depth', 'height'))
- new_second: float32 [2, 110592], P(None, ('dp', 'depth', 'height'))
The draws below stay inside these ranges and needn't reach their ends.
All inputs are finite; a program needn't handle non-finite values.
Results may differ from the reference program's by a relative error of at most 0.0095.
The reference program's roundings to bfloat16 on the way (of `kernels`, `hidden`, `delta_two` and `delta_one`) count: a program that leaves them out, or rounds other values in their place, can miss the bound.
Values may be sent and summed in bfloat16 or wider, within the bound.
A program may use at most 192 MiB of HBM per device.

```python
import math
import jax
import jax.numpy as jnp
from jax import lax

C = 64
WIDTH = 64
LAYERS = 2
VOLUMES = 2
DEPTH = 8
HEIGHT = 32
WSIZE = 110592


def steps_of(own_key, shape, shards, smallest, high):
    gain = 1.0
    for axis_at, blocks in shards:
        steps = jax.random.uniform(jax.random.fold_in(jax.random.fold_in(own_key, 6), axis_at), (blocks,), jnp.float32, smallest / len(shards), high / len(shards))
        gain = gain * jnp.repeat(jnp.exp(steps), shape[axis_at] // blocks).reshape((-1,) + (1,) * (len(shape) - 1 - axis_at))
    return gain


def gaussian(stream_key, extent, spread, reach, split=(), kind=jnp.bfloat16):
    drawn = spread * jax.random.normal(stream_key, extent, jnp.float32)
    if split:
        drawn = drawn * steps_of(stream_key, extent, split, -0.22, 0.18)
    return jnp.clip(drawn, -reach, reach).astype(kind)


def setup_inputs(seed: int = 0) -> dict:
    keys = jax.random.split(jax.random.key(seed), 6)
    return {
        "volume": gaussian(keys[0], (VOLUMES, DEPTH, HEIGHT, WIDTH * C), 1.0, 6.0, ((0, 2), (1, 4), (2, 4))),
        "feature_grad": gaussian(keys[1], (VOLUMES, DEPTH, HEIGHT, WIDTH * C), (4.0 / (VOLUMES * DEPTH * HEIGHT * WIDTH) ** 0.5), 0.125, ((0, 2), (1, 4), (2, 4))),
        "master_weights": gaussian(keys[2], (LAYERS, WSIZE), (27 * C) ** -0.5, 0.15625, ((1, 32),), jnp.float32),
        "first_moment": gaussian(keys[3], (LAYERS, WSIZE), 0.5, 3.0, ((1, 32),), jnp.float32),
        "second_moment": jnp.clip(jnp.exp(math.log(4.0) - 3.6888794 * jax.random.uniform(keys[4], (LAYERS, WSIZE), jnp.float32) ** steps_of(keys[4], (LAYERS, WSIZE), ((1, 32),), -0.2, 0.2)), 0.1, 4.0),
    }


leak_slope = 0.3
first_decay = 0.9
second_decay = 0.999
learn_rate = 0.001
epsilon = 1e-08
step_count = 10

def convolve(inputs, kernel):
    return lax.conv_general_dilated(inputs[None], kernel.reshape(3, 3, 3, C, C), (1, 1, 1), ((1, 1), (1, 1), (1, 1)), dimension_numbers=('NDHWC', 'DHWIO', 'NDHWC'), precision=lax.Precision.HIGHEST)[0]

def slope_of(linear):
    return jnp.where(linear > 0, 1.0, leak_slope)

def reference(volume, feature_grad, master_weights, first_moment, second_moment):
    rounded = lax.optimization_barrier(master_weights.astype(jnp.bfloat16))
    kernels = rounded.astype(jnp.float32)
    kernel_one = kernels[0]
    kernel_two = kernels[1]

    def per_volume(totals, volume_pair):
        one_volume, one_grad = volume_pair
        inputs = one_volume.reshape(DEPTH, HEIGHT, WIDTH, C).astype(jnp.float32)
        linear_one = convolve(inputs, kernel_one)
        hidden_low = lax.optimization_barrier((linear_one * slope_of(linear_one)).astype(jnp.bfloat16))
        hidden = hidden_low.astype(jnp.float32)
        linear_two = convolve(hidden, kernel_two)
        features = (linear_two * slope_of(linear_two)).astype(jnp.bfloat16)
        delta_low = lax.optimization_barrier((one_grad.reshape(DEPTH, HEIGHT, WIDTH, C).astype(jnp.float32) * slope_of(linear_two)).astype(jnp.bfloat16))
        delta_two = delta_low.astype(jnp.float32)
        unused, pull_two = jax.vjp(convolve, hidden, kernel_two)
        back_one, grad_two = pull_two(delta_two)
        delta_one_low = lax.optimization_barrier((back_one * slope_of(linear_one)).astype(jnp.bfloat16))
        delta_one = delta_one_low.astype(jnp.float32)
        unused_one, pull_one = jax.vjp(lambda kernel: convolve(inputs, kernel), kernel_one)
        grad_one = pull_one(delta_one)[0]
        return ((totals[0] + grad_one, totals[1] + grad_two), features.reshape(DEPTH, HEIGHT, WIDTH * C))
    empty_grad = jnp.zeros((WSIZE,), jnp.float32)
    summed, features = lax.scan(per_volume, (empty_grad, empty_grad), (volume, feature_grad))
    grads = jnp.stack([summed[0], summed[1]])
    new_first = first_decay * first_moment + (1.0 - first_decay) * grads
    new_second = second_decay * second_moment + (1.0 - second_decay) * grads * grads
    first_fix = 1.0 - first_decay ** step_count
    second_fix = 1.0 - second_decay ** step_count
    new_weights = master_weights - learn_rate * (new_first / first_fix) / (jnp.sqrt(new_second / second_fix) + epsilon)
    return (features, new_weights, new_first, new_second)
```

```python
import functools

import jax
import jax.numpy as jnp
from jax import lax
from jax.experimental import pallas as pl
from jax.experimental.pallas import tpu as pltpu
from jax.sharding import PartitionSpec as P

C = 64
WIDTH = 64

leak_slope = 0.3
first_decay = 0.9
second_decay = 0.999
learn_rate = 0.001
epsilon = 1e-08
step_count = 10

MESH = pl.DeviceIdType.MESH
BF = jnp.bfloat16
F32 = jnp.float32
SIDES = [(a, b) for a in (-1, 0, 1) for b in (-1, 0, 1) if (a, b) != (0, 0)]


def bit_plan(sizes):
    dp, depth, height = sizes
    plan = []
    for k in range(height.bit_length() - 1):
        plan.append((2, 1 << k))
    for k in range(1, depth.bit_length() - 1):
        plan.append((1, 1 << k))
    for k in range(dp.bit_length() - 1):
        plan.append((0, 1 << k))
    plan.append((1, 1))
    return plan


def place_of(plan):
    index = [lax.axis_index("dp"), lax.axis_index("depth"), lax.axis_index("height")]
    bits, partners = [], []
    for axis, unit in plan:
        bit = lax.rem(index[axis] // unit, 2)
        other = list(index)
        other[axis] = index[axis] + (1 - 2 * bit) * unit
        bits.append(bit)
        partners.append(tuple(other))
    return bits, partners


def greet(partners):
    barrier = pltpu.get_barrier_semaphore()
    for partner in partners:
        pl.semaphore_signal(barrier, inc=1, device_id=partner, device_id_type=MESH)
    pl.semaphore_wait(barrier, len(partners))


def gather_kernel(plan, own_ref, all_ref, send_sem, recv_sem):
    bits, partners = place_of(plan)
    place = sum(bit * (1 << k) for k, bit in enumerate(bits))
    greet(partners)
    all_ref[pl.ds(place, 1)] = own_ref[...].astype(BF)[None]
    for k, partner in enumerate(partners):
        size = 1 << k
        start = (place // size) * size
        copy = pltpu.make_async_remote_copy(
            src_ref=all_ref.at[pl.ds(start, size)],
            dst_ref=all_ref.at[pl.ds(start, size)],
            send_sem=send_sem.at[k],
            recv_sem=recv_sem.at[k],
            device_id=partner,
            device_id_type=MESH,
        )
        copy.start()
        copy.wait()


def scatter_kernel(plan, grads_ref, out_ref, acc, outgoing, incoming, send_sem, recv_sem):
    bits, partners = place_of(plan)
    greet(partners)
    base = 0
    for k in reversed(range(len(plan))):
        size = 1 << k
        source = grads_ref if k == len(plan) - 1 else acc
        give = base + (1 - bits[k]) * size
        keep = base + bits[k] * size
        outgoing[pl.ds(size, size)] = source[pl.ds(give, size)].astype(BF)
        copy = pltpu.make_async_remote_copy(
            src_ref=outgoing.at[pl.ds(size, size)],
            dst_ref=incoming.at[pl.ds(size, size)],
            send_sem=send_sem.at[k],
            recv_sem=recv_sem.at[k],
            device_id=partners[k],
            device_id_type=MESH,
        )
        copy.start()
        copy.wait()
        total = source[pl.ds(keep, size)] + incoming[pl.ds(size, size)].astype(F32)
        if k:
            acc[pl.ds(keep, size)] = total
        else:
            out_ref[...] = total[0]
        base = keep


def span(side, cells, arriving):
    if side == 0:
        return pl.ds(1, cells)
    if side < 0:
        return pl.ds(cells + 1 if arriving else 1, 1)
    return pl.ds(0 if arriving else cells, 1)


def shifted(x, step, w):
    rolled = pltpu.roll(x, step % x.shape[0], 0)
    edge = 0 if step == 1 else WIDTH - 1
    return jnp.where(w == edge, 0.0, rolled)


def layers_kernel(
    depth_n,
    height_n,
    vol_ref,
    fg_ref,
    w1_ref,
    w2_ref,
    wb_ref,
    feat_ref,
    grad_ref,
    vol,
    hid,
    del2,
    wide_v,
    wide_h,
    slope1,
    slots,
    send_sem,
    recv_sem,
):
    cells_d, cells_h = vol_ref.shape[0], vol_ref.shape[1]
    rows = cells_d * cells_h * WIDTH
    me_p, me_d, me_h = lax.axis_index("dp"), lax.axis_index("depth"), lax.axis_index("height")
    own = (pl.ds(1, cells_d), pl.ds(1, cells_h))

    def there(a, b):
        d, h = me_d + a, me_h + b
        return (d >= 0) & (d < depth_n) & (h >= 0) & (h < height_n)

    for buffer in (vol, hid, del2):
        for d in (0, cells_d + 1):
            buffer[d] = jnp.zeros_like(buffer[d])
        for h in (0, cells_h + 1):
            buffer[pl.ds(1, cells_d), h] = jnp.zeros((cells_d, WIDTH, C), BF)
    vol[own] = vol_ref[...]

    barrier = pltpu.get_barrier_semaphore()
    for a, b in SIDES:

        @pl.when(there(a, b))
        def _(a=a, b=b):
            pl.semaphore_signal(
                barrier, inc=1, device_id=(me_p, me_d + a, me_h + b), device_id_type=MESH
            )

    near_d = 1 + jnp.where(me_d > 0, 1, 0) + jnp.where(me_d < depth_n - 1, 1, 0)
    near_h = 1 + jnp.where(me_h > 0, 1, 0) + jnp.where(me_h < height_n - 1, 1, 0)
    pl.semaphore_wait(barrier, near_d * near_h - 1)

    def copy_of(buffer, which, n):
        a, b = SIDES[n]
        return pltpu.make_async_remote_copy(
            src_ref=buffer.at[span(a, cells_d, False), span(b, cells_h, False)],
            dst_ref=buffer.at[span(a, cells_d, True), span(b, cells_h, True)],
            send_sem=send_sem.at[which, n],
            recv_sem=recv_sem.at[which, n],
            device_id=(me_p, me_d + a, me_h + b),
            device_id_type=MESH,
        )

    def send(buffer, which):
        for n, (a, b) in enumerate(SIDES):

            @pl.when(there(a, b))
            def _(n=n):
                copy_of(buffer, which, n).start()

    def arrive(buffer, which):
        for n, (a, b) in enumerate(SIDES):

            @pl.when(there(-a, -b))
            def _(n=n):
                copy_of(buffer, which, n).wait_recv()

    def sent(buffer, which):
        for n, (a, b) in enumerate(SIDES):

            @pl.when(there(a, b))
            def _(n=n):
                copy_of(buffer, which, n).wait_send()

    def widen(buffer, wide):
        for b in range(3):
            wide[:, :, :, pl.ds(b * C, C)] = buffer[:, pl.ds(b, cells_h)]

    w_of = lax.broadcasted_iota(jnp.int32, (rows // cells_d, C), 0) % WIDTH

    def conv(wide, weights_ref, d):
        total = None
        for a in range(3):
            term = jnp.dot(
                wide[d + a].reshape(cells_h * WIDTH, 3 * C),
                weights_ref[a],
                preferred_element_type=F32,
            )
            total = term if total is None else total + term
        return (
            shifted(total[:, 0:C], 1, w_of)
            + total[:, C : 2 * C]
            + shifted(total[:, 2 * C : 3 * C], -1, w_of)
        )

    def tripled(delta):
        wide = delta.reshape(cells_d, cells_h * WIDTH, C)
        for d in range(cells_d):
            slots[pl.ds(d * cells_h * WIDTH, cells_h * WIDTH), pl.ds(0, C)] = shifted(
                wide[d], -1, w_of
            ).astype(BF)
            slots[pl.ds(d * cells_h * WIDTH, cells_h * WIDTH), pl.ds(C, C)] = wide[d].astype(BF)
            slots[pl.ds(d * cells_h * WIDTH, cells_h * WIDTH), pl.ds(2 * C, C)] = shifted(
                wide[d], 1, w_of
            ).astype(BF)

    def grad(wide, layer):
        for a in range(3):
            grad_ref[layer, a] = lax.dot_general(
                wide[a : a + cells_d].reshape(rows, 3 * C),
                slots[...],
                (((0,), (0,)), ((), ())),
                preferred_element_type=F32,
            )

    send(vol, 0)
    arrive(vol, 0)
    widen(vol, wide_v)
    for d in range(cells_d):
        linear = conv(wide_v, w1_ref, d)
        slope = jnp.where(linear > 0, 1.0, leak_slope)
        slope1[d] = slope
        hid[d + 1, pl.ds(1, cells_h)] = (linear * slope).astype(BF).reshape(cells_h, WIDTH, C)
    send(hid, 1)
    arrive(hid, 1)
    widen(hid, wide_h)
    for d in range(cells_d):
        linear = conv(wide_h, w2_ref, d)
        slope = jnp.where(linear > 0, 1.0, leak_slope)
        feat_ref[d] = (linear * slope).astype(BF).reshape(cells_h, WIDTH, C)
        given = fg_ref[d].astype(F32).reshape(cells_h * WIDTH, C)
        del2[d + 1, pl.ds(1, cells_h)] = (given * slope).astype(BF).reshape(cells_h, WIDTH, C)
    send(del2, 2)
    tripled(del2[own].astype(F32).reshape(rows, C))
    grad(wide_h, 1)
    arrive(del2, 2)
    widen(del2, wide_h)
    deltas = [conv(wide_h, wb_ref, d) * slope1[d] for d in range(cells_d)]
    tripled(jnp.concatenate(deltas, 0).astype(BF).astype(F32))
    grad(wide_v, 0)
    for which, buffer in enumerate((vol, hid, del2)):
        sent(buffer, which)


def vmem(count):
    return [pl.BlockSpec(memory_space=pltpu.VMEM)] * count


def body(sizes, volume, feature_grad, master_weights, first_moment, second_moment):
    dp_n, depth_n, height_n = sizes
    devices = dp_n * depth_n * height_n
    plan = bit_plan(sizes)
    steps = len(plan)
    cells_d, cells_h = volume.shape[1], volume.shape[2]
    shard = master_weights.shape[1]
    slot_rows = -(-2 * shard // (16 * 128)) * 16
    pad = slot_rows * 128 - 2 * shard

    slot = jnp.pad(master_weights.reshape(-1), (0, pad)).reshape(slot_rows, 128)
    gathered = pl.pallas_call(
        functools.partial(gather_kernel, plan),
        out_shape=jax.ShapeDtypeStruct((devices, slot_rows, 128), BF),
        in_specs=vmem(1),
        out_specs=vmem(1)[0],
        scratch_shapes=[pltpu.SemaphoreType.DMA((steps,)), pltpu.SemaphoreType.DMA((steps,))],
        compiler_params=pltpu.CompilerParams(
            collective_id=0, has_side_effects=True, vmem_limit_bytes=32 * 2**20
        ),
        name="gather_kernels",
    )(slot)
    gathered = gathered.reshape(2, dp_n, depth_n // 2, height_n, slot_rows * 128)[..., : 2 * shard]
    kernels = (
        gathered.reshape(2, dp_n, depth_n // 2, height_n, 2, shard)
        .transpose(4, 1, 2, 0, 3, 5)
        .reshape(2, 3, 3, 3, C, C)
    )
    forward = kernels.transpose(0, 1, 2, 4, 3, 5).reshape(2, 3, 3 * C, 3 * C)
    back = kernels[1, ::-1, ::-1, ::-1].transpose(0, 1, 4, 2, 3).reshape(3, 3 * C, 3 * C)

    block = (cells_d, cells_h, WIDTH, C)
    padded = (cells_d + 2, cells_h + 2, WIDTH, C)
    wide = (cells_d + 2, cells_h, WIDTH, 3 * C)
    features, grads = pl.pallas_call(
        functools.partial(layers_kernel, depth_n, height_n),
        out_shape=(
            jax.ShapeDtypeStruct(block, BF),
            jax.ShapeDtypeStruct((2, 3, 3 * C, 3 * C), F32),
        ),
        in_specs=vmem(5),
        out_specs=tuple(vmem(2)),
        scratch_shapes=[
            pltpu.VMEM(padded, BF),
            pltpu.VMEM(padded, BF),
            pltpu.VMEM(padded, BF),
            pltpu.VMEM(wide, BF),
            pltpu.VMEM(wide, BF),
            pltpu.VMEM((cells_d, cells_h * WIDTH, C), F32),
            pltpu.VMEM((cells_d * cells_h * WIDTH, 3 * C), BF),
            pltpu.SemaphoreType.DMA((3, 8)),
            pltpu.SemaphoreType.DMA((3, 8)),
        ],
        compiler_params=pltpu.CompilerParams(
            collective_id=1, has_side_effects=True, vmem_limit_bytes=48 * 2**20
        ),
        name="two_layers",
    )(volume.reshape(block), feature_grad.reshape(block), forward[0], forward[1], back)
    features = features.reshape(1, cells_d, cells_h, WIDTH * C)

    parts = (
        grads.reshape(2, 3, 3, C, 3, C)
        .transpose(0, 1, 2, 4, 3, 5)
        .reshape(2, dp_n, depth_n // 2, 2, height_n, shard)
        .transpose(3, 1, 2, 4, 0, 5)
        .reshape(devices, 2 * shard)
    )
    parts = jnp.pad(parts, ((0, 0), (0, pad))).reshape(devices, slot_rows, 128)
    summed = pl.pallas_call(
        functools.partial(scatter_kernel, plan),
        out_shape=jax.ShapeDtypeStruct((slot_rows, 128), F32),
        in_specs=vmem(1),
        out_specs=vmem(1)[0],
        scratch_shapes=[
            pltpu.VMEM((devices, slot_rows, 128), F32),
            pltpu.VMEM((devices, slot_rows, 128), BF),
            pltpu.VMEM((devices, slot_rows, 128), BF),
            pltpu.SemaphoreType.DMA((steps,)),
            pltpu.SemaphoreType.DMA((steps,)),
        ],
        compiler_params=pltpu.CompilerParams(
            collective_id=2, has_side_effects=True, vmem_limit_bytes=32 * 2**20
        ),
        name="scatter_grads",
    )(parts)
    summed = summed.reshape(-1)[: 2 * shard].reshape(2, shard)

    new_first = first_decay * first_moment + (1.0 - first_decay) * summed
    new_second = second_decay * second_moment + (1.0 - second_decay) * summed * summed
    first_fix = 1.0 - first_decay**step_count
    second_fix = 1.0 - second_decay**step_count
    new_weights = master_weights - learn_rate * (new_first / first_fix) / (
        jnp.sqrt(new_second / second_fix) + epsilon
    )
    return (features, new_weights, new_first, new_second)


def solution(mesh):
    sizes = (mesh.shape["dp"], mesh.shape["depth"], mesh.shape["height"])
    owners = P(None, ("dp", "depth", "height"))
    blocks = P("dp", "depth", "height", None)
    return jax.shard_map(
        functools.partial(body, sizes),
        mesh=mesh,
        in_specs=(blocks, blocks, owners, owners, owners),
        out_specs=(blocks, owners, owners, owners),
        check_vma=False,
    )
```

```python
import functools

import jax
import jax.numpy as jnp
from jax import lax
from jax.experimental import pallas as pl
from jax.experimental.pallas import tpu as pltpu
from jax.sharding import PartitionSpec as P

C = 64
WIDTH = 64

leak_slope = 0.3
first_decay = 0.9
second_decay = 0.999
learn_rate = 0.001
epsilon = 1e-08
step_count = 10

MESH = pl.DeviceIdType.MESH
BF = jnp.bfloat16
F32 = jnp.float32
SIDES = [(a, b) for a in (-1, 0, 1) for b in (-1, 0, 1) if (a, b) != (0, 0)]


def bit_plan(sizes):
    dp, depth, height = sizes
    plan = []
    for k in range(height.bit_length() - 1):
        plan.append((2, 1 << k))
    for k in range(1, depth.bit_length() - 1):
        plan.append((1, 1 << k))
    for k in range(dp.bit_length() - 1):
        plan.append((0, 1 << k))
    plan.append((1, 1))
    return plan


def place_of(plan):
    index = [lax.axis_index("dp"), lax.axis_index("depth"), lax.axis_index("height")]
    bits, partners = [], []
    for axis, unit in plan:
        bit = lax.rem(index[axis] // unit, 2)
        other = list(index)
        other[axis] = index[axis] + (1 - 2 * bit) * unit
        bits.append(bit)
        partners.append(tuple(other))
    return bits, partners


def greet(partners):
    barrier = pltpu.get_barrier_semaphore()
    for partner in partners:
        pl.semaphore_signal(barrier, inc=1, device_id=partner, device_id_type=MESH)
    pl.semaphore_wait(barrier, len(partners))


def gather_kernel(
    plan, depth_n, height_n, own_ref, vol_ref, all_ref, wide_ref, vol, send_sem, recv_sem, side_send, side_recv
):
    bits, partners = place_of(plan)
    place = sum(bit * (1 << k) for k, bit in enumerate(bits))
    there, count, id_of = neighbours(depth_n, height_n)
    clear_edges(vol)
    vol[pl.ds(1, vol_ref.shape[0]), pl.ds(1, vol_ref.shape[1])] = vol_ref[...]
    all_ref[pl.ds(place, 1)] = own_ref[...].astype(BF)[None]
    barrier = signal_neighbours(there, id_of)
    for partner in partners:
        pl.semaphore_signal(barrier, inc=1, device_id=partner, device_id_type=MESH)
    pl.semaphore_wait(barrier, count + len(partners))
    halo = Halo(vol, there, id_of, side_send, side_recv)
    for k, partner in enumerate(partners):
        size = 1 << k
        start = (place // size) * size
        copy = pltpu.make_async_remote_copy(
            src_ref=all_ref.at[pl.ds(start, size)],
            dst_ref=all_ref.at[pl.ds(start, size)],
            send_sem=send_sem.at[k],
            recv_sem=recv_sem.at[k],
            device_id=partner,
            device_id_type=MESH,
        )
        copy.start()
        if k == 0:
            halo.send()
        if k == len(partners) - 1:
            halo.arrive()
            widen(vol, wide_ref)
        copy.wait()
    halo.sent()


def scatter_kernel(plan, grads_ref, out_ref, acc, outgoing, incoming, send_sem, recv_sem):
    bits, partners = place_of(plan)
    greet(partners)
    base = 0
    for k in reversed(range(len(plan))):
        size = 1 << k
        source = grads_ref if k == len(plan) - 1 else acc
        give = base + (1 - bits[k]) * size
        keep = base + bits[k] * size
        outgoing[pl.ds(size, size)] = source[pl.ds(give, size)].astype(BF)
        copy = pltpu.make_async_remote_copy(
            src_ref=outgoing.at[pl.ds(size, size)],
            dst_ref=incoming.at[pl.ds(size, size)],
            send_sem=send_sem.at[k],
            recv_sem=recv_sem.at[k],
            device_id=partners[k],
            device_id_type=MESH,
        )
        copy.start()
        copy.wait()
        total = source[pl.ds(keep, size)] + incoming[pl.ds(size, size)].astype(F32)
        if k:
            acc[pl.ds(keep, size)] = total
        else:
            out_ref[...] = total[0]
        base = keep


def span(side, cells, arriving):
    if side == 0:
        return pl.ds(1, cells)
    if side < 0:
        return pl.ds(cells + 1 if arriving else 1, 1)
    return pl.ds(0 if arriving else cells, 1)


def shifted(x, step, w):
    rolled = pltpu.roll(x, step % x.shape[0], 0)
    edge = 0 if step == 1 else WIDTH - 1
    return jnp.where(w == edge, 0.0, rolled)


def neighbours(depth_n, height_n):
    me_p, me_d, me_h = lax.axis_index("dp"), lax.axis_index("depth"), lax.axis_index("height")

    def there(a, b):
        d, h = me_d + a, me_h + b
        return (d >= 0) & (d < depth_n) & (h >= 0) & (h < height_n)

    near_d = 1 + jnp.where(me_d > 0, 1, 0) + jnp.where(me_d < depth_n - 1, 1, 0)
    near_h = 1 + jnp.where(me_h > 0, 1, 0) + jnp.where(me_h < height_n - 1, 1, 0)
    return there, near_d * near_h - 1, lambda a, b: (me_p, me_d + a, me_h + b)


def signal_neighbours(there, id_of):
    barrier = pltpu.get_barrier_semaphore()
    for a, b in SIDES:

        @pl.when(there(a, b))
        def _(a=a, b=b):
            pl.semaphore_signal(barrier, inc=1, device_id=id_of(a, b), device_id_type=MESH)

    return barrier


def clear_edges(buffer):
    depth, height = buffer.shape[0], buffer.shape[1]
    for d in (0, depth - 1):
        buffer[d] = jnp.zeros_like(buffer[d])
    for h in (0, height - 1):
        buffer[pl.ds(1, depth - 2), h] = jnp.zeros((depth - 2, WIDTH, C), BF)


class Halo:
    def __init__(self, buffer, there, id_of, send_sem, recv_sem):
        self.there, self.copies = there, []
        depth, height = buffer.shape[0] - 2, buffer.shape[1] - 2
        for n, (a, b) in enumerate(SIDES):

            def make(n=n, a=a, b=b):
                return pltpu.make_async_remote_copy(
                    src_ref=buffer.at[span(a, depth, False), span(b, height, False)],
                    dst_ref=buffer.at[span(a, depth, True), span(b, height, True)],
                    send_sem=send_sem.at[n],
                    recv_sem=recv_sem.at[n],
                    device_id=id_of(a, b),
                    device_id_type=MESH,
                )

            self.copies.append(make)

    def each(self, sign, act):
        for make, (a, b) in zip(self.copies, SIDES):

            @pl.when(self.there(sign * a, sign * b))
            def _(make=make):
                act(make())

    def send(self):
        self.each(1, lambda copy: copy.start())

    def arrive(self):
        self.each(-1, lambda copy: copy.wait_recv())

    def sent(self):
        self.each(1, lambda copy: copy.wait_send())


def widen(buffer, wide):
    for b in range(3):
        wide[:, :, :, pl.ds(b * C, C)] = buffer[:, pl.ds(b, wide.shape[1])]


def layers_kernel(
    depth_n,
    height_n,
    wide_v,
    fg_ref,
    kern_ref,
    feat_ref,
    grad_ref,
    hid,
    del2,
    wide_h,
    slope1,
    slots,
    weights,
    mixed,
    send_sem,
    recv_sem,
):
    cells_d, cells_h = fg_ref.shape[0], fg_ref.shape[1]
    line = cells_h * WIDTH
    there, count, id_of = neighbours(depth_n, height_n)
    clear_edges(hid)
    clear_edges(del2)
    barrier = signal_neighbours(there, id_of)

    half = C // 2
    for layer in range(2):
        for a in range(3):
            for b in range(3):
                taps = [
                    kern_ref[layer, pl.ds((9 * a + 3 * b + c) * half, half)].astype(F32)
                    for c in range(3)
                ]
                for odd in range(2):
                    at = pl.ds(b * C + odd, half, stride=2)
                    parts = [tap[:, odd * C : (odd + 1) * C] for tap in taps]
                    mixed[a, 0, at, :] = jnp.concatenate(parts[:2], 1)
                    mixed[a, 1, at, :] = jnp.concatenate([parts[2], parts[2]], 1)
            weights[layer, a, :, 0 : 2 * C] = mixed[a, 0].astype(BF)
            weights[layer, a, :, 2 * C : 3 * C] = mixed[a, 1, :, 0:C].astype(BF)

    pl.semaphore_wait(barrier, count)
    hid_halo = Halo(hid, there, id_of, send_sem.at[0], recv_sem.at[0])
    del_halo = Halo(del2, there, id_of, send_sem.at[1], recv_sem.at[1])

    def width_of(rows):
        return lax.broadcasted_iota(jnp.int32, (rows, C), 0) % WIDTH

    def conv(wide, layer, d):
        total = None
        for a in range(3):
            term = jnp.dot(
                wide[d + a].reshape(line, 3 * C), weights[layer, a], preferred_element_type=F32
            )
            total = term if total is None else total + term
        w = width_of(line)
        return (
            shifted(total[:, 0:C], 1, w)
            + total[:, C : 2 * C]
            + shifted(total[:, 2 * C : 3 * C], -1, w)
        )

    def triple(d, first, layers, delta):
        rows = layers * WIDTH
        w = width_of(rows)
        delta = delta.astype(F32).reshape(rows, C)
        at = pl.ds(first * WIDTH, rows)
        slots[d, at, pl.ds(0, C)] = shifted(delta, -1, w).astype(BF)
        slots[d, at, pl.ds(C, C)] = delta.astype(BF)
        slots[d, at, pl.ds(2 * C, C)] = shifted(delta, 1, w).astype(BF)

    def grad(wide, layer):
        tripled = slots[pl.ds(1, cells_d), pl.ds(WIDTH, line)].reshape(cells_d * line, 3 * C)
        for a in range(3):
            result = lax.dot_general(
                wide[a : a + cells_d].reshape(cells_d * line, 3 * C),
                tripled,
                (((0,), (0,)), ((), ())),
                preferred_element_type=F32,
            )
            mixed[a, 0] = result[:, 0 : 2 * C]
            mixed[a, 1, :, 0:C] = result[:, 2 * C : 3 * C]
            even, odd = (
                [mixed[a, n, pl.ds(first, 3 * half, stride=2), :] for n in range(2)]
                for first in range(2)
            )
            for b in range(3):
                for c in range(3):
                    part = (slice(b * half, (b + 1) * half), slice(c % 2 * C, (c % 2 + 1) * C))
                    grad_ref[layer, pl.ds((9 * a + 3 * b + c) * half, half)] = jnp.concatenate(
                        [even[c // 2][part], odd[c // 2][part]], 1
                    )

    for d in range(cells_d):
        linear = conv(wide_v, 0, d)
        slope = jnp.where(linear > 0, 1.0, leak_slope)
        slope1[d] = slope
        hid[d + 1, pl.ds(1, cells_h)] = (linear * slope).astype(BF).reshape(cells_h, WIDTH, C)
    hid_halo.send()
    hid_halo.arrive()
    widen(hid, wide_h)
    for d in range(cells_d):
        linear = conv(wide_h, 1, d)
        slope = jnp.where(linear > 0, 1.0, leak_slope)
        feat_ref[d] = (linear * slope).astype(BF).reshape(cells_h, WIDTH, C)
        given = fg_ref[d].astype(F32).reshape(line, C)
        del2[d + 1, pl.ds(1, cells_h)] = (given * slope).astype(BF).reshape(cells_h, WIDTH, C)
    del_halo.send()
    for d in range(1, cells_d + 1):
        triple(d, 1, cells_h, del2[d, pl.ds(1, cells_h)])
    grad(wide_h, 1)
    del_halo.arrive()
    for d in range(cells_d + 2):
        if d in (0, cells_d + 1):
            triple(d, 0, cells_h + 2, del2[d])
        else:
            triple(d, 0, 1, del2[d, 0])
            triple(d, cells_h + 1, 1, del2[d, cells_h + 1])
    deltas = []
    for d in range(cells_d):
        total = None
        for a in range(3):
            spread = lax.dot_general(
                slots[d + 2 - a],
                weights[1, a],
                (((1,), (1,)), ((), ())),
                preferred_element_type=F32,
            )
            for b in range(3):
                term = spread[(2 - b) * WIDTH : (2 - b) * WIDTH + line, b * C : (b + 1) * C]
                total = term if total is None else total + term
        deltas.append((total * slope1[d]).astype(BF))
    for d in range(cells_d):
        triple(d + 1, 1, cells_h, deltas[d])
    grad(wide_v, 0)
    hid_halo.sent()
    del_halo.sent()


def vmem(count):
    return [pl.BlockSpec(memory_space=pltpu.VMEM)] * count


def body(sizes, volume, feature_grad, master_weights, first_moment, second_moment):
    dp_n, depth_n, height_n = sizes
    devices = dp_n * depth_n * height_n
    plan = bit_plan(sizes)
    steps = len(plan)
    cells_d, cells_h = volume.shape[1], volume.shape[2]
    shard = master_weights.shape[1]
    slot_rows = -(-2 * shard // (16 * 128)) * 16
    pad = slot_rows * 128 - 2 * shard

    slot = jnp.pad(master_weights.reshape(-1), (0, pad)).reshape(slot_rows, 128)
    block = (cells_d, cells_h, WIDTH, C)
    padded = (cells_d + 2, cells_h + 2, WIDTH, C)
    wide = (cells_d + 2, cells_h, WIDTH, 3 * C)
    gathered, wide_volume = pl.pallas_call(
        functools.partial(gather_kernel, plan, depth_n, height_n),
        out_shape=(
            jax.ShapeDtypeStruct((devices, slot_rows, 128), BF),
            jax.ShapeDtypeStruct(wide, BF),
        ),
        in_specs=vmem(2),
        out_specs=tuple(vmem(2)),
        scratch_shapes=[
            pltpu.VMEM(padded, BF),
            pltpu.SemaphoreType.DMA((steps,)),
            pltpu.SemaphoreType.DMA((steps,)),
            pltpu.SemaphoreType.DMA((8,)),
            pltpu.SemaphoreType.DMA((8,)),
        ],
        compiler_params=pltpu.CompilerParams(
            collective_id=0, has_side_effects=True, vmem_limit_bytes=32 * 2**20
        ),
        name="gather_kernels",
    )(slot, volume.reshape(block))
    if shard % 128 == 0:
        unit = (shard // 128, 128)
        gathered = gathered[:, : 2 * shard // 128]
    else:
        unit = (shard,)
        gathered = gathered.reshape(devices, slot_rows * 128)[:, : 2 * shard]
    order = (4, 1, 2, 0, 3) + tuple(range(5, 5 + len(unit)))
    kernels = (
        gathered.reshape((2, dp_n, depth_n // 2, height_n, 2) + unit)
        .transpose(order)
        .reshape(2, devices * shard // 128, 128)
    )

    features, grads = pl.pallas_call(
        functools.partial(layers_kernel, depth_n, height_n),
        out_shape=(
            jax.ShapeDtypeStruct(block, BF),
            jax.ShapeDtypeStruct(kernels.shape, F32),
        ),
        in_specs=vmem(3),
        out_specs=tuple(vmem(2)),
        scratch_shapes=[
            pltpu.VMEM(padded, BF),
            pltpu.VMEM(padded, BF),
            pltpu.VMEM(wide, BF),
            pltpu.VMEM((cells_d, cells_h * WIDTH, C), F32),
            pltpu.VMEM((cells_d + 2, (cells_h + 2) * WIDTH, 3 * C), BF),
            pltpu.VMEM((2, 3, 3 * C, 3 * C), BF),
            pltpu.VMEM((3, 2, 3 * C, 2 * C), F32),
            pltpu.SemaphoreType.DMA((2, 8)),
            pltpu.SemaphoreType.DMA((2, 8)),
        ],
        compiler_params=pltpu.CompilerParams(
            collective_id=1, has_side_effects=True, vmem_limit_bytes=48 * 2**20
        ),
        name="two_layers",
    )(wide_volume, feature_grad.reshape(block), kernels)
    features = features.reshape(1, cells_d, cells_h, WIDTH * C)

    order = (3, 1, 2, 4, 0) + tuple(range(5, 5 + len(unit)))
    parts = grads.reshape((2, dp_n, depth_n // 2, 2, height_n) + unit).transpose(order)
    if len(unit) == 2:
        parts = parts.reshape(devices, 2 * unit[0], 128)
        parts = jnp.pad(parts, ((0, 0), (0, slot_rows - 2 * unit[0]), (0, 0)))
    else:
        parts = jnp.pad(parts.reshape(devices, 2 * shard), ((0, 0), (0, pad)))
        parts = parts.reshape(devices, slot_rows, 128)
    summed = pl.pallas_call(
        functools.partial(scatter_kernel, plan),
        out_shape=jax.ShapeDtypeStruct((slot_rows, 128), F32),
        in_specs=vmem(1),
        out_specs=vmem(1)[0],
        scratch_shapes=[
            pltpu.VMEM((devices, slot_rows, 128), F32),
            pltpu.VMEM((devices, slot_rows, 128), BF),
            pltpu.VMEM((devices, slot_rows, 128), BF),
            pltpu.SemaphoreType.DMA((steps,)),
            pltpu.SemaphoreType.DMA((steps,)),
        ],
        compiler_params=pltpu.CompilerParams(
            collective_id=2, has_side_effects=True, vmem_limit_bytes=32 * 2**20
        ),
        name="scatter_grads",
    )(parts)
    summed = summed.reshape(-1)[: 2 * shard].reshape(2, shard)

    new_first = first_decay * first_moment + (1.0 - first_decay) * summed
    new_second = second_decay * second_moment + (1.0 - second_decay) * summed * summed
    first_fix = 1.0 - first_decay**step_count
    second_fix = 1.0 - second_decay**step_count
    new_weights = master_weights - learn_rate * (new_first / first_fix) / (
        jnp.sqrt(new_second / second_fix) + epsilon
    )
    return (features, new_weights, new_first, new_second)


def solution(mesh):
    sizes = (mesh.shape["dp"], mesh.shape["depth"], mesh.shape["height"])
    owners = P(None, ("dp", "depth", "height"))
    blocks = P("dp", "depth", "height", None)
    return jax.shard_map(
        functools.partial(body, sizes),
        mesh=mesh,
        in_specs=(blocks, blocks, owners, owners, owners),
        out_specs=(blocks, owners, owners, owners),
        check_vma=False,
    )
```

```python
import functools

import jax
import jax.numpy as jnp
from jax import lax
from jax.experimental import pallas as pl
from jax.experimental.pallas import tpu as pltpu
from jax.sharding import PartitionSpec as P

C = 64
WIDTH = 64

leak_slope = 0.3
first_decay = 0.9
second_decay = 0.999
learn_rate = 0.001
epsilon = 1e-08
step_count = 10

MESH = pl.DeviceIdType.MESH
BF = jnp.bfloat16
F32 = jnp.float32
SIDES = [(a, b) for a in (-1, 0, 1) for b in (-1, 0, 1) if (a, b) != (0, 0)]


class Groups:
    def __init__(self, sizes):
        dp, depth, height = sizes
        self.line, self.group = height, dp * (depth // 2)
        self.half = self.line * self.group
        p, d, h = lax.axis_index("dp"), lax.axis_index("depth"), lax.axis_index("height")
        pairs = depth // 2
        self.h, self.core = h, lax.rem(d, 2)
        self.q = p * pairs + d // 2
        self.start = self.core * self.half + self.q * self.line
        self.in_line = [
            (lax.rem(h + r, height), lax.rem(h + height - r, height)) for r in range(1, height)
        ]
        self.in_group = [
            (lax.rem(self.q + r, self.group), lax.rem(self.q + self.group - r, self.group))
            for r in range(1, self.group)
        ]
        self.line_ids = [(p, d, to) for to, _ in self.in_line]
        self.group_ids = [
            (to // pairs, 2 * lax.rem(to, pairs) + self.core, h) for to, _ in self.in_group
        ]
        self.core_id = (p, d + 1 - 2 * self.core, h)
        self.ids = self.line_ids + self.group_ids + [self.core_id]

    def greet(self):
        barrier = pltpu.get_barrier_semaphore()
        for other in self.ids:
            pl.semaphore_signal(barrier, inc=1, device_id=other, device_id_type=MESH)
        return barrier, len(self.ids)


def gather_kernel(
    sizes,
    own_ref,
    vol_ref,
    all_ref,
    wide_ref,
    vol,
    send_sem,
    recv_sem,
    side_send,
    side_recv,
):
    at = Groups(sizes)
    there, count, id_of = neighbours(sizes[1], sizes[2])
    clear_edges(vol)
    vol[pl.ds(1, vol_ref.shape[0]), pl.ds(1, vol_ref.shape[1])] = vol_ref[...]
    all_ref[pl.ds(at.start + at.h, 1)] = own_ref[...].astype(BF)[None]
    barrier, partners = at.greet()
    signal_neighbours(there, id_of)
    pl.semaphore_wait(barrier, count + partners)
    halo = Halo(vol, there, id_of, side_send, side_recv)

    def copy_of(n, place, size):
        part = all_ref.at[pl.ds(place, size)]
        return pltpu.make_async_remote_copy(
            src_ref=part,
            dst_ref=part,
            send_sem=send_sem.at[n],
            recv_sem=recv_sem.at[n],
            device_id=at.ids[n],
            device_id_type=MESH,
        )

    mine = at.core * at.half
    others = (1 - at.core) * at.half
    phases = [
        [(at.start + at.h, at.start + source, 1) for _, source in at.in_line],
        [(at.start, mine + source * at.line, at.line) for _, source in at.in_group],
        [(mine, others, at.half)],
    ]
    first = 0
    for number, phase in enumerate(phases):
        for n, (out, _, size) in enumerate(phase):
            copy_of(first + n, out, size).start()
        if number == 0:
            halo.send()
        if number == 2:
            halo.arrive()
            widen(vol, wide_ref)
        for n, (_, source, size) in enumerate(phase):
            copy_of(first + n, source, size).wait_recv()
        first += len(phase)
    first = 0
    for phase in phases:
        for n, (out, _, size) in enumerate(phase):
            copy_of(first + n, out, size).wait_send()
        first += len(phase)
    halo.sent()


def scatter_kernel(sizes, grads_ref, out_ref, acc, outgoing, incoming, send_sem, recv_sem):
    at = Groups(sizes)
    barrier, partners = at.greet()
    line, half = at.line, at.half

    def copy_of(n, source, place, size):
        return pltpu.make_async_remote_copy(
            src_ref=outgoing.at[pl.ds(source, size)],
            dst_ref=incoming.at[pl.ds(place, size)],
            send_sem=send_sem.at[n],
            recv_sem=recv_sem.at[n],
            device_id=at.ids[n],
            device_id_type=MESH,
        )

    last = len(at.ids) - 1
    outgoing[pl.ds(half, half)] = grads_ref[pl.ds((1 - at.core) * half, half)].astype(BF)
    pl.semaphore_wait(barrier, partners)
    across = copy_of(last, half, half, half)
    across.start()
    across.wait_recv()
    total = grads_ref[pl.ds(at.core * half, half)] + incoming[pl.ds(half, half)].astype(F32)
    acc[...] = total
    outgoing[pl.ds(0, half)] = total.astype(BF)
    first = len(at.in_line)
    copies = [across]
    group = []
    for n, (to, _) in enumerate(at.in_group):
        group.append(copy_of(first + n, to * line, (n + 1) * line, line))
        group[-1].start()
    total = acc[pl.ds(at.q * line, line)]
    for n, copy in enumerate(group):
        copy.wait_recv()
        total = total + incoming[pl.ds((n + 1) * line, line)].astype(F32)
    acc[pl.ds(at.q * line, line)] = total
    outgoing[pl.ds(at.q * line, line)] = total.astype(BF)
    final = []
    for n, (to, _) in enumerate(at.in_line):
        final.append(copy_of(n, at.q * line + to, n + 1, 1))
        final[-1].start()
    total = acc[pl.ds(at.q * line + at.h, 1)]
    for n, copy in enumerate(final):
        copy.wait_recv()
        total = total + incoming[pl.ds(n + 1, 1)].astype(F32)
    out_ref[...] = total[0]
    for copy in copies + group + final:
        copy.wait_send()


def span(side, cells, arriving):
    if side == 0:
        return pl.ds(1, cells)
    if side < 0:
        return pl.ds(cells + 1 if arriving else 1, 1)
    return pl.ds(0 if arriving else cells, 1)


def shifted(x, step, w):
    rolled = pltpu.roll(x, step % x.shape[0], 0)
    edge = 0 if step == 1 else WIDTH - 1
    return jnp.where(w == edge, 0.0, rolled)


def neighbours(depth_n, height_n):
    me_p, me_d, me_h = lax.axis_index("dp"), lax.axis_index("depth"), lax.axis_index("height")

    def there(a, b):
        d, h = me_d + a, me_h + b
        return (d >= 0) & (d < depth_n) & (h >= 0) & (h < height_n)

    near_d = 1 + jnp.where(me_d > 0, 1, 0) + jnp.where(me_d < depth_n - 1, 1, 0)
    near_h = 1 + jnp.where(me_h > 0, 1, 0) + jnp.where(me_h < height_n - 1, 1, 0)
    return there, near_d * near_h - 1, lambda a, b: (me_p, me_d + a, me_h + b)


def signal_neighbours(there, id_of):
    barrier = pltpu.get_barrier_semaphore()
    for a, b in SIDES:

        @pl.when(there(a, b))
        def _(a=a, b=b):
            pl.semaphore_signal(barrier, inc=1, device_id=id_of(a, b), device_id_type=MESH)

    return barrier


def clear_edges(buffer):
    depth, height = buffer.shape[0], buffer.shape[1]
    for d in (0, depth - 1):
        buffer[d] = jnp.zeros_like(buffer[d])
    for h in (0, height - 1):
        buffer[pl.ds(1, depth - 2), h] = jnp.zeros((depth - 2, WIDTH, C), BF)


class Halo:
    def __init__(self, buffer, there, id_of, send_sem, recv_sem):
        self.there, self.copies = there, []
        depth, height = buffer.shape[0] - 2, buffer.shape[1] - 2
        for n, (a, b) in enumerate(SIDES):

            def make(n=n, a=a, b=b):
                return pltpu.make_async_remote_copy(
                    src_ref=buffer.at[span(a, depth, False), span(b, height, False)],
                    dst_ref=buffer.at[span(a, depth, True), span(b, height, True)],
                    send_sem=send_sem.at[n],
                    recv_sem=recv_sem.at[n],
                    device_id=id_of(a, b),
                    device_id_type=MESH,
                )

            self.copies.append(make)

    def each(self, sign, act):
        for make, (a, b) in zip(self.copies, SIDES):

            @pl.when(self.there(sign * a, sign * b))
            def _(make=make):
                act(make())

    def send(self):
        self.each(1, lambda copy: copy.start())

    def arrive(self):
        self.each(-1, lambda copy: copy.wait_recv())

    def sent(self):
        self.each(1, lambda copy: copy.wait_send())


def widen(buffer, wide):
    for b in range(3):
        wide[:, :, :, pl.ds(b * C, C)] = buffer[:, pl.ds(b, wide.shape[1])]


def layers_kernel(
    depth_n,
    height_n,
    wide_v,
    fg_ref,
    kern_ref,
    feat_ref,
    grad_ref,
    hid,
    del2,
    wide_h,
    slope1,
    slots,
    weights,
    mixed,
    send_sem,
    recv_sem,
):
    cells_d, cells_h = fg_ref.shape[0], fg_ref.shape[1]
    line = cells_h * WIDTH
    there, count, id_of = neighbours(depth_n, height_n)
    clear_edges(hid)
    clear_edges(del2)
    barrier = signal_neighbours(there, id_of)

    half = C // 2
    for layer in range(2):
        for a in range(3):
            for b in range(3):
                taps = [
                    kern_ref[layer, pl.ds((9 * a + 3 * b + c) * half, half)].astype(F32)
                    for c in range(3)
                ]
                for odd in range(2):
                    at = pl.ds(b * C + odd, half, stride=2)
                    parts = [tap[:, odd * C : (odd + 1) * C] for tap in taps]
                    mixed[a, 0, at, :] = jnp.concatenate(parts[:2], 1)
                    mixed[a, 1, at, :] = jnp.concatenate([parts[2], parts[2]], 1)
            weights[layer, a, :, 0 : 2 * C] = mixed[a, 0].astype(BF)
            weights[layer, a, :, 2 * C : 3 * C] = mixed[a, 1, :, 0:C].astype(BF)

    pl.semaphore_wait(barrier, count)
    hid_halo = Halo(hid, there, id_of, send_sem.at[0], recv_sem.at[0])
    del_halo = Halo(del2, there, id_of, send_sem.at[1], recv_sem.at[1])

    def width_of(rows):
        return lax.broadcasted_iota(jnp.int32, (rows, C), 0) % WIDTH

    def conv(wide, layer, d):
        total = None
        for a in range(3):
            term = jnp.dot(
                wide[d + a].reshape(line, 3 * C), weights[layer, a], preferred_element_type=F32
            )
            total = term if total is None else total + term
        w = width_of(line)
        return (
            shifted(total[:, 0:C], 1, w)
            + total[:, C : 2 * C]
            + shifted(total[:, 2 * C : 3 * C], -1, w)
        )

    def triple(d, first, layers, delta):
        rows = layers * WIDTH
        w = width_of(rows)
        delta = delta.astype(F32).reshape(rows, C)
        at = pl.ds(first * WIDTH, rows)
        slots[d, at, pl.ds(0, C)] = shifted(delta, -1, w).astype(BF)
        slots[d, at, pl.ds(C, C)] = delta.astype(BF)
        slots[d, at, pl.ds(2 * C, C)] = shifted(delta, 1, w).astype(BF)

    def grad(wide, layer):
        tripled = slots[pl.ds(1, cells_d), pl.ds(WIDTH, line)].reshape(cells_d * line, 3 * C)
        for a in range(3):
            result = lax.dot_general(
                wide[a : a + cells_d].reshape(cells_d * line, 3 * C),
                tripled,
                (((0,), (0,)), ((), ())),
                preferred_element_type=F32,
            )
            mixed[a, 0] = result[:, 0 : 2 * C]
            mixed[a, 1, :, 0:C] = result[:, 2 * C : 3 * C]
            even, odd = (
                [mixed[a, n, pl.ds(first, 3 * half, stride=2), :] for n in range(2)]
                for first in range(2)
            )
            for b in range(3):
                for c in range(3):
                    part = (slice(b * half, (b + 1) * half), slice(c % 2 * C, (c % 2 + 1) * C))
                    grad_ref[layer, pl.ds((9 * a + 3 * b + c) * half, half)] = jnp.concatenate(
                        [even[c // 2][part], odd[c // 2][part]], 1
                    )

    for d in range(cells_d):
        linear = conv(wide_v, 0, d)
        slope = jnp.where(linear > 0, 1.0, leak_slope)
        slope1[d] = slope
        hid[d + 1, pl.ds(1, cells_h)] = (linear * slope).astype(BF).reshape(cells_h, WIDTH, C)
    hid_halo.send()
    hid_halo.arrive()
    widen(hid, wide_h)
    for d in range(cells_d):
        linear = conv(wide_h, 1, d)
        slope = jnp.where(linear > 0, 1.0, leak_slope)
        feat_ref[d] = (linear * slope).astype(BF).reshape(cells_h, WIDTH, C)
        given = fg_ref[d].astype(F32).reshape(line, C)
        del2[d + 1, pl.ds(1, cells_h)] = (given * slope).astype(BF).reshape(cells_h, WIDTH, C)
    del_halo.send()
    for d in range(1, cells_d + 1):
        triple(d, 1, cells_h, del2[d, pl.ds(1, cells_h)])
    grad(wide_h, 1)
    del_halo.arrive()
    for d in range(cells_d + 2):
        if d in (0, cells_d + 1):
            triple(d, 0, cells_h + 2, del2[d])
        else:
            triple(d, 0, 1, del2[d, 0])
            triple(d, cells_h + 1, 1, del2[d, cells_h + 1])
    deltas = []
    for d in range(cells_d):
        total = None
        for a in range(3):
            spread = lax.dot_general(
                slots[d + 2 - a],
                weights[1, a],
                (((1,), (1,)), ((), ())),
                preferred_element_type=F32,
            )
            for b in range(3):
                term = spread[(2 - b) * WIDTH : (2 - b) * WIDTH + line, b * C : (b + 1) * C]
                total = term if total is None else total + term
        deltas.append((total * slope1[d]).astype(BF))
    for d in range(cells_d):
        triple(d + 1, 1, cells_h, deltas[d])
    grad(wide_v, 0)
    hid_halo.sent()
    del_halo.sent()


def vmem(count):
    return [pl.BlockSpec(memory_space=pltpu.VMEM)] * count


def body(sizes, volume, feature_grad, master_weights, first_moment, second_moment):
    dp_n, depth_n, height_n = sizes
    devices = dp_n * depth_n * height_n
    steps = (height_n - 1) + (dp_n * (depth_n // 2) - 1) + 1
    cells_d, cells_h = volume.shape[1], volume.shape[2]
    shard = master_weights.shape[1]
    slot_rows = -(-2 * shard // (16 * 128)) * 16
    pad = slot_rows * 128 - 2 * shard

    slot = jnp.pad(master_weights.reshape(-1), (0, pad)).reshape(slot_rows, 128)
    block = (cells_d, cells_h, WIDTH, C)
    padded = (cells_d + 2, cells_h + 2, WIDTH, C)
    wide = (cells_d + 2, cells_h, WIDTH, 3 * C)
    gathered, wide_volume = pl.pallas_call(
        functools.partial(gather_kernel, sizes),
        out_shape=(
            jax.ShapeDtypeStruct((devices, slot_rows, 128), BF),
            jax.ShapeDtypeStruct(wide, BF),
        ),
        in_specs=vmem(2),
        out_specs=tuple(vmem(2)),
        scratch_shapes=[
            pltpu.VMEM(padded, BF),
            pltpu.SemaphoreType.DMA((steps,)),
            pltpu.SemaphoreType.DMA((steps,)),
            pltpu.SemaphoreType.DMA((8,)),
            pltpu.SemaphoreType.DMA((8,)),
        ],
        compiler_params=pltpu.CompilerParams(
            collective_id=0, has_side_effects=True, vmem_limit_bytes=32 * 2**20
        ),
        name="gather_kernels",
    )(slot, volume.reshape(block))
    if shard % 128 == 0:
        unit = (shard // 128, 128)
        gathered = gathered[:, : 2 * shard // 128]
    else:
        unit = (shard,)
        gathered = gathered.reshape(devices, slot_rows * 128)[:, : 2 * shard]
    order = (4, 1, 2, 0, 3) + tuple(range(5, 5 + len(unit)))
    kernels = (
        gathered.reshape((2, dp_n, depth_n // 2, height_n, 2) + unit)
        .transpose(order)
        .reshape(2, devices * shard // 128, 128)
    )

    features, grads = pl.pallas_call(
        functools.partial(layers_kernel, depth_n, height_n),
        out_shape=(
            jax.ShapeDtypeStruct(block, BF),
            jax.ShapeDtypeStruct(kernels.shape, F32),
        ),
        in_specs=vmem(3),
        out_specs=tuple(vmem(2)),
        scratch_shapes=[
            pltpu.VMEM(padded, BF),
            pltpu.VMEM(padded, BF),
            pltpu.VMEM(wide, BF),
            pltpu.VMEM((cells_d, cells_h * WIDTH, C), F32),
            pltpu.VMEM((cells_d + 2, (cells_h + 2) * WIDTH, 3 * C), BF),
            pltpu.VMEM((2, 3, 3 * C, 3 * C), BF),
            pltpu.VMEM((3, 2, 3 * C, 2 * C), F32),
            pltpu.SemaphoreType.DMA((2, 8)),
            pltpu.SemaphoreType.DMA((2, 8)),
        ],
        compiler_params=pltpu.CompilerParams(
            collective_id=1, has_side_effects=True, vmem_limit_bytes=48 * 2**20
        ),
        name="two_layers",
    )(wide_volume, feature_grad.reshape(block), kernels)
    features = features.reshape(1, cells_d, cells_h, WIDTH * C)

    order = (3, 1, 2, 4, 0) + tuple(range(5, 5 + len(unit)))
    parts = grads.reshape((2, dp_n, depth_n // 2, 2, height_n) + unit).transpose(order)
    if len(unit) == 2:
        parts = parts.reshape(devices, 2 * unit[0], 128)
        parts = jnp.pad(parts, ((0, 0), (0, slot_rows - 2 * unit[0]), (0, 0)))
    else:
        parts = jnp.pad(parts.reshape(devices, 2 * shard), ((0, 0), (0, pad)))
        parts = parts.reshape(devices, slot_rows, 128)
    summed = pl.pallas_call(
        functools.partial(scatter_kernel, sizes),
        out_shape=jax.ShapeDtypeStruct((slot_rows, 128), F32),
        in_specs=vmem(1),
        out_specs=vmem(1)[0],
        scratch_shapes=[
            pltpu.VMEM((devices // 2, slot_rows, 128), F32),
            pltpu.VMEM((devices, slot_rows, 128), BF),
            pltpu.VMEM((devices, slot_rows, 128), BF),
            pltpu.SemaphoreType.DMA((steps,)),
            pltpu.SemaphoreType.DMA((steps,)),
        ],
        compiler_params=pltpu.CompilerParams(
            collective_id=2, has_side_effects=True, vmem_limit_bytes=32 * 2**20
        ),
        name="scatter_grads",
    )(parts)
    summed = summed.reshape(-1)[: 2 * shard].reshape(2, shard)

    new_first = first_decay * first_moment + (1.0 - first_decay) * summed
    new_second = second_decay * second_moment + (1.0 - second_decay) * summed * summed
    first_fix = 1.0 - first_decay**step_count
    second_fix = 1.0 - second_decay**step_count
    new_weights = master_weights - learn_rate * (new_first / first_fix) / (
        jnp.sqrt(new_second / second_fix) + epsilon
    )
    return (features, new_weights, new_first, new_second)


def solution(mesh):
    sizes = (mesh.shape["dp"], mesh.shape["depth"], mesh.shape["height"])
    owners = P(None, ("dp", "depth", "height"))
    blocks = P("dp", "depth", "height", None)
    return jax.shard_map(
        functools.partial(body, sizes),
        mesh=mesh,
        in_specs=(blocks, blocks, owners, owners, owners),
        out_specs=(blocks, owners, owners, owners),
        check_vma=False,
    )
```

```python
import functools

import jax
import jax.numpy as jnp
from jax import lax
from jax.experimental import pallas as pl
from jax.experimental.pallas import tpu as pltpu
from jax.sharding import PartitionSpec as P

C = 64
WIDTH = 64

leak_slope = 0.3
first_decay = 0.9
second_decay = 0.999
learn_rate = 0.001
epsilon = 1e-08
step_count = 10

MESH = pl.DeviceIdType.MESH
BF = jnp.bfloat16
F32 = jnp.float32
SIDES = [(a, b) for a in (-1, 0, 1) for b in (-1, 0, 1) if (a, b) != (0, 0)]


class Groups:
    def __init__(self, sizes):
        dp, depth, height = sizes
        self.line, self.group = height, dp * (depth // 2)
        self.half = self.line * self.group
        p, d, h = lax.axis_index("dp"), lax.axis_index("depth"), lax.axis_index("height")
        pairs = depth // 2
        self.h, self.core = h, lax.rem(d, 2)
        self.q = p * pairs + d // 2
        self.start = self.core * self.half + self.q * self.line
        self.in_line = [
            (lax.rem(h + r, height), lax.rem(h + height - r, height)) for r in range(1, height)
        ]
        self.in_group = [
            (lax.rem(self.q + r, self.group), lax.rem(self.q + self.group - r, self.group))
            for r in range(1, self.group)
        ]
        self.line_ids = [(p, d, to) for to, _ in self.in_line]
        self.group_ids = [
            (to // pairs, 2 * lax.rem(to, pairs) + self.core, h) for to, _ in self.in_group
        ]
        self.core_id = (p, d + 1 - 2 * self.core, h)
        self.ids = self.line_ids + self.group_ids + [self.core_id]
        self.peers = self.line_ids + self.group_ids + [self.core_id] * self.group

    def greet(self):
        barrier = pltpu.get_barrier_semaphore()
        for other in self.ids:
            pl.semaphore_signal(barrier, inc=1, device_id=other, device_id_type=MESH)
        return barrier, len(self.ids)


def gather_kernel(
    sizes,
    own_ref,
    vol_ref,
    all_ref,
    wide_ref,
    vol,
    send_sem,
    recv_sem,
    side_send,
    side_recv,
):
    at = Groups(sizes)
    there, count, id_of = neighbours(sizes[1], sizes[2])
    clear_edges(vol)
    vol[pl.ds(1, vol_ref.shape[0]), pl.ds(1, vol_ref.shape[1])] = vol_ref[...]
    all_ref[pl.ds(at.start + at.h, 1)] = own_ref[...].astype(BF)[None]
    barrier, partners = at.greet()
    signal_neighbours(there, id_of)
    pl.semaphore_wait(barrier, count + partners)
    halo = Halo(vol, there, id_of, side_send, side_recv)

    def copy_of(n, place, size):
        part = all_ref.at[pl.ds(place, size)]
        return pltpu.make_async_remote_copy(
            src_ref=part,
            dst_ref=part,
            send_sem=send_sem.at[n],
            recv_sem=recv_sem.at[n],
            device_id=at.peers[n],
            device_id_type=MESH,
        )

    mine = at.core * at.half
    others = (1 - at.core) * at.half
    line = at.line
    sent = []

    def start(n, place, size):
        sent.append(copy_of(n, place, size))
        sent[-1].start()

    for n in range(len(at.in_line)):
        start(n, at.start + at.h, 1)
    halo.send()
    for n, (_, source) in enumerate(at.in_line):
        copy_of(n, at.start + source, 1).wait_recv()
    first = len(at.in_line)
    core = first + len(at.in_group)
    for n in range(len(at.in_group)):
        start(first + n, at.start, line)
    start(core, at.start, line)
    for n, (_, source) in enumerate(at.in_group):
        copy_of(first + n, mine + source * line, line).wait_recv()
        start(core + 1 + n, mine + source * line, line)
    halo.arrive()
    widen(vol, wide_ref)
    for n, source in enumerate([at.q] + [source for _, source in at.in_group]):
        copy_of(core + n, others + source * line, line).wait_recv()
    for copy in sent:
        copy.wait_send()
    halo.sent()


def scatter_kernel(sizes, grads_ref, out_ref, acc, outgoing, incoming, send_sem, recv_sem):
    at = Groups(sizes)
    barrier, partners = at.greet()
    line, half = at.line, at.half

    def copy_of(n, source, place, size):
        return pltpu.make_async_remote_copy(
            src_ref=outgoing.at[pl.ds(source, size)],
            dst_ref=incoming.at[pl.ds(place, size)],
            send_sem=send_sem.at[n],
            recv_sem=recv_sem.at[n],
            device_id=at.peers[n],
            device_id_type=MESH,
        )

    first = len(at.in_line)
    core = first + len(at.in_group)
    order = [to for to, _ in at.in_group] + [at.q]
    keep, give = at.core * half, (1 - at.core) * half
    pl.semaphore_wait(barrier, partners)
    across = []
    for n, to in enumerate(order):
        there = half + to * line
        outgoing[pl.ds(there, line)] = grads_ref[pl.ds(give + to * line, line)].astype(BF)
        across.append(copy_of(core + n, there, there, line))
        across[-1].start()
    group = []
    for n, to in enumerate(order):
        across[n].wait_recv()
        total = grads_ref[pl.ds(keep + to * line, line)]
        total = total + incoming[pl.ds(half + to * line, line)].astype(F32)
        if n < len(at.in_group):
            outgoing[pl.ds(to * line, line)] = total.astype(BF)
            group.append(copy_of(first + n, to * line, (n + 1) * line, line))
            group[-1].start()
    for n, copy in enumerate(group):
        copy.wait_recv()
        total = total + incoming[pl.ds((n + 1) * line, line)].astype(F32)
    acc[...] = total
    outgoing[pl.ds(at.q * line, line)] = total.astype(BF)
    final = []
    for n, (to, _) in enumerate(at.in_line):
        final.append(copy_of(n, at.q * line + to, n + 1, 1))
        final[-1].start()
    total = acc[pl.ds(at.h, 1)]
    for n, copy in enumerate(final):
        copy.wait_recv()
        total = total + incoming[pl.ds(n + 1, 1)].astype(F32)
    out_ref[...] = total[0]
    for copy in across + group + final:
        copy.wait_send()


def span(side, cells, arriving):
    if side == 0:
        return pl.ds(1, cells)
    if side < 0:
        return pl.ds(cells + 1 if arriving else 1, 1)
    return pl.ds(0 if arriving else cells, 1)


def shifted(x, step, w):
    rolled = pltpu.roll(x, step % x.shape[0], 0)
    edge = 0 if step == 1 else WIDTH - 1
    return jnp.where(w == edge, 0.0, rolled)


def neighbours(depth_n, height_n):
    me_p, me_d, me_h = lax.axis_index("dp"), lax.axis_index("depth"), lax.axis_index("height")

    def there(a, b):
        d, h = me_d + a, me_h + b
        return (d >= 0) & (d < depth_n) & (h >= 0) & (h < height_n)

    near_d = 1 + jnp.where(me_d > 0, 1, 0) + jnp.where(me_d < depth_n - 1, 1, 0)
    near_h = 1 + jnp.where(me_h > 0, 1, 0) + jnp.where(me_h < height_n - 1, 1, 0)
    return there, near_d * near_h - 1, lambda a, b: (me_p, me_d + a, me_h + b)


def signal_neighbours(there, id_of):
    barrier = pltpu.get_barrier_semaphore()
    for a, b in SIDES:

        @pl.when(there(a, b))
        def _(a=a, b=b):
            pl.semaphore_signal(barrier, inc=1, device_id=id_of(a, b), device_id_type=MESH)

    return barrier


def clear_edges(buffer):
    depth, height = buffer.shape[0], buffer.shape[1]
    for d in (0, depth - 1):
        buffer[d] = jnp.zeros_like(buffer[d])
    for h in (0, height - 1):
        buffer[pl.ds(1, depth - 2), h] = jnp.zeros((depth - 2, WIDTH, C), BF)


class Halo:
    def __init__(self, buffer, there, id_of, send_sem, recv_sem):
        self.there, self.copies = there, []
        depth, height = buffer.shape[0] - 2, buffer.shape[1] - 2
        for n, (a, b) in enumerate(SIDES):

            def make(n=n, a=a, b=b):
                return pltpu.make_async_remote_copy(
                    src_ref=buffer.at[span(a, depth, False), span(b, height, False)],
                    dst_ref=buffer.at[span(a, depth, True), span(b, height, True)],
                    send_sem=send_sem.at[n],
                    recv_sem=recv_sem.at[n],
                    device_id=id_of(a, b),
                    device_id_type=MESH,
                )

            self.copies.append(make)

    def each(self, sign, act):
        for make, (a, b) in zip(self.copies, SIDES):

            @pl.when(self.there(sign * a, sign * b))
            def _(make=make):
                act(make())

    def send(self):
        self.each(1, lambda copy: copy.start())

    def arrive(self):
        self.each(-1, lambda copy: copy.wait_recv())

    def sent(self):
        self.each(1, lambda copy: copy.wait_send())


def widen(buffer, wide):
    for b in range(3):
        wide[:, :, :, pl.ds(b * C, C)] = buffer[:, pl.ds(b, wide.shape[1])]


def layers_kernel(
    depth_n,
    height_n,
    slot_of,
    wide_v,
    fg_ref,
    kern_ref,
    feat_ref,
    grad_ref,
    hid,
    del2,
    wide_h,
    slope1,
    slots,
    weights,
    mixed,
    send_sem,
    recv_sem,
):
    cells_d, cells_h = fg_ref.shape[0], fg_ref.shape[1]
    line = cells_h * WIDTH
    there, count, id_of = neighbours(depth_n, height_n)
    if slot_of is not None:
        used = 2 * slot_of[1]
        spare = (grad_ref.shape[0], grad_ref.shape[1] - used, 128)
        grad_ref[:, pl.ds(used, spare[1])] = jnp.zeros(spare, F32)
    clear_edges(hid)
    clear_edges(del2)
    barrier = signal_neighbours(there, id_of)

    half = C // 2
    for layer in range(2):
        for a in range(3):
            for b in range(3):
                taps = [
                    kern_ref[layer, pl.ds((9 * a + 3 * b + c) * half, half)].astype(F32)
                    for c in range(3)
                ]
                for odd in range(2):
                    at = pl.ds(b * C + odd, half, stride=2)
                    parts = [tap[:, odd * C : (odd + 1) * C] for tap in taps]
                    mixed[a, 0, at, :] = jnp.concatenate(parts[:2], 1)
                    mixed[a, 1, at, :] = jnp.concatenate([parts[2], parts[2]], 1)
            weights[layer, a, :, 0 : 2 * C] = mixed[a, 0].astype(BF)
            weights[layer, a, :, 2 * C : 3 * C] = mixed[a, 1, :, 0:C].astype(BF)

    pl.semaphore_wait(barrier, count)
    hid_halo = Halo(hid, there, id_of, send_sem.at[0], recv_sem.at[0])
    del_halo = Halo(del2, there, id_of, send_sem.at[1], recv_sem.at[1])

    def width_of(rows):
        return lax.broadcasted_iota(jnp.int32, (rows, C), 0) % WIDTH

    def conv(wide, layer, d):
        total = None
        for a in range(3):
            term = jnp.dot(
                wide[d + a].reshape(line, 3 * C), weights[layer, a], preferred_element_type=F32
            )
            total = term if total is None else total + term
        w = width_of(line)
        return (
            shifted(total[:, 0:C], 1, w)
            + total[:, C : 2 * C]
            + shifted(total[:, 2 * C : 3 * C], -1, w)
        )

    def triple(d, first, layers, delta):
        rows = layers * WIDTH
        w = width_of(rows)
        delta = delta.astype(F32).reshape(rows, C)
        at = pl.ds(first * WIDTH, rows)
        slots[d, at, pl.ds(0, C)] = shifted(delta, -1, w).astype(BF)
        slots[d, at, pl.ds(C, C)] = delta.astype(BF)
        slots[d, at, pl.ds(2 * C, C)] = shifted(delta, 1, w).astype(BF)

    def grad(wide, layer):
        tripled = slots[pl.ds(1, cells_d), pl.ds(WIDTH, line)].reshape(cells_d * line, 3 * C)
        for a in range(3):
            result = lax.dot_general(
                wide[a : a + cells_d].reshape(cells_d * line, 3 * C),
                tripled,
                (((0,), (0,)), ((), ())),
                preferred_element_type=F32,
            )
            mixed[a, 0] = result[:, 0 : 2 * C]
            mixed[a, 1, :, 0:C] = result[:, 2 * C : 3 * C]
            even, odd = (
                [mixed[a, n, pl.ds(first, 3 * half, stride=2), :] for n in range(2)]
                for first in range(2)
            )
            for b in range(3):
                for c in range(3):
                    part = (slice(b * half, (b + 1) * half), slice(c % 2 * C, (c % 2 + 1) * C))
                    tap = jnp.concatenate([even[c // 2][part], odd[c // 2][part]], 1)
                    row = (9 * a + 3 * b + c) * half
                    if slot_of is None:
                        grad_ref[layer, pl.ds(row, half)] = tap
                        continue
                    at, share = 0, slot_of[1]
                    while at < half:
                        owner, skip = divmod(row + at, share)
                        size = min(half - at, share - skip)
                        grad_ref[slot_of[0][owner], pl.ds(layer * share + skip, size)] = tap[
                            at : at + size
                        ]
                        at += size

    for d in range(cells_d):
        linear = conv(wide_v, 0, d)
        slope = jnp.where(linear > 0, 1.0, leak_slope)
        slope1[d] = slope
        hid[d + 1, pl.ds(1, cells_h)] = (linear * slope).astype(BF).reshape(cells_h, WIDTH, C)
    hid_halo.send()
    hid_halo.arrive()
    widen(hid, wide_h)
    for d in range(cells_d):
        linear = conv(wide_h, 1, d)
        slope = jnp.where(linear > 0, 1.0, leak_slope)
        feat_ref[d] = (linear * slope).astype(BF).reshape(cells_h, WIDTH, C)
        given = fg_ref[d].astype(F32).reshape(line, C)
        del2[d + 1, pl.ds(1, cells_h)] = (given * slope).astype(BF).reshape(cells_h, WIDTH, C)
    del_halo.send()
    for d in range(1, cells_d + 1):
        triple(d, 1, cells_h, del2[d, pl.ds(1, cells_h)])
    grad(wide_h, 1)
    del_halo.arrive()
    for d in range(cells_d + 2):
        if d in (0, cells_d + 1):
            triple(d, 0, cells_h + 2, del2[d])
        else:
            triple(d, 0, 1, del2[d, 0])
            triple(d, cells_h + 1, 1, del2[d, cells_h + 1])
    deltas = []
    for d in range(cells_d):
        total = None
        for a in range(3):
            spread = lax.dot_general(
                slots[d + 2 - a],
                weights[1, a],
                (((1,), (1,)), ((), ())),
                preferred_element_type=F32,
            )
            for b in range(3):
                term = spread[(2 - b) * WIDTH : (2 - b) * WIDTH + line, b * C : (b + 1) * C]
                total = term if total is None else total + term
        deltas.append((total * slope1[d]).astype(BF))
    for d in range(cells_d):
        triple(d + 1, 1, cells_h, deltas[d])
    grad(wide_v, 0)
    hid_halo.sent()
    del_halo.sent()


def vmem(count):
    return [pl.BlockSpec(memory_space=pltpu.VMEM)] * count


def body(sizes, volume, feature_grad, master_weights, first_moment, second_moment):
    dp_n, depth_n, height_n = sizes
    devices = dp_n * depth_n * height_n
    steps = (height_n - 1) + 2 * dp_n * (depth_n // 2) - 1
    cells_d, cells_h = volume.shape[1], volume.shape[2]
    shard = master_weights.shape[1]
    slot_rows = -(-2 * shard // (16 * 128)) * 16
    pad = slot_rows * 128 - 2 * shard

    slot = jnp.pad(master_weights.reshape(-1), (0, pad)).reshape(slot_rows, 128)
    block = (cells_d, cells_h, WIDTH, C)
    padded = (cells_d + 2, cells_h + 2, WIDTH, C)
    wide = (cells_d + 2, cells_h, WIDTH, 3 * C)
    gathered, wide_volume = pl.pallas_call(
        functools.partial(gather_kernel, sizes),
        out_shape=(
            jax.ShapeDtypeStruct((devices, slot_rows, 128), BF),
            jax.ShapeDtypeStruct(wide, BF),
        ),
        in_specs=vmem(2),
        out_specs=tuple(vmem(2)),
        scratch_shapes=[
            pltpu.VMEM(padded, BF),
            pltpu.SemaphoreType.DMA((steps,)),
            pltpu.SemaphoreType.DMA((steps,)),
            pltpu.SemaphoreType.DMA((8,)),
            pltpu.SemaphoreType.DMA((8,)),
        ],
        compiler_params=pltpu.CompilerParams(
            collective_id=0, has_side_effects=True, vmem_limit_bytes=32 * 2**20
        ),
        name="gather_kernels",
    )(slot, volume.reshape(block))
    if shard % 128 == 0:
        unit = (shard // 128, 128)
        gathered = gathered[:, : 2 * shard // 128]
    else:
        unit = (shard,)
        gathered = gathered.reshape(devices, slot_rows * 128)[:, : 2 * shard]
    order = (4, 1, 2, 0, 3) + tuple(range(5, 5 + len(unit)))
    kernels = (
        gathered.reshape((2, dp_n, depth_n // 2, height_n, 2) + unit)
        .transpose(order)
        .reshape(2, devices * shard // 128, 128)
    )

    slot_of, grads_shape = None, kernels.shape
    if len(unit) == 2 and slot_rows > 2 * unit[0]:
        places = []
        for device in range(devices):
            p, d, h = device // (depth_n * height_n), device // height_n % depth_n, device % height_n
            places.append(((d % 2 * dp_n + p) * (depth_n // 2) + d // 2) * height_n + h)
        slot_of, grads_shape = (places, unit[0]), (devices, slot_rows, 128)

    features, grads = pl.pallas_call(
        functools.partial(layers_kernel, depth_n, height_n, slot_of),
        out_shape=(
            jax.ShapeDtypeStruct(block, BF),
            jax.ShapeDtypeStruct(grads_shape, F32),
        ),
        in_specs=vmem(3),
        out_specs=tuple(vmem(2)),
        scratch_shapes=[
            pltpu.VMEM(padded, BF),
            pltpu.VMEM(padded, BF),
            pltpu.VMEM(wide, BF),
            pltpu.VMEM((cells_d, cells_h * WIDTH, C), F32),
            pltpu.VMEM((cells_d + 2, (cells_h + 2) * WIDTH, 3 * C), BF),
            pltpu.VMEM((2, 3, 3 * C, 3 * C), BF),
            pltpu.VMEM((3, 2, 3 * C, 2 * C), F32),
            pltpu.SemaphoreType.DMA((2, 8)),
            pltpu.SemaphoreType.DMA((2, 8)),
        ],
        compiler_params=pltpu.CompilerParams(
            collective_id=1, has_side_effects=True, vmem_limit_bytes=48 * 2**20
        ),
        name="two_layers",
    )(wide_volume, feature_grad.reshape(block), kernels)
    features = features.reshape(1, cells_d, cells_h, WIDTH * C)

    order = (3, 1, 2, 4, 0) + tuple(range(5, 5 + len(unit)))
    if slot_of is None:
        parts = grads.reshape((2, dp_n, depth_n // 2, 2, height_n) + unit).transpose(order)
    if slot_of is not None:
        parts = grads
    elif len(unit) == 2:
        parts = parts.reshape(devices, 2 * unit[0], 128)
        parts = jnp.pad(parts, ((0, 0), (0, slot_rows - 2 * unit[0]), (0, 0)))
    else:
        parts = jnp.pad(parts.reshape(devices, 2 * shard), ((0, 0), (0, pad)))
        parts = parts.reshape(devices, slot_rows, 128)
    summed = pl.pallas_call(
        functools.partial(scatter_kernel, sizes),
        out_shape=jax.ShapeDtypeStruct((slot_rows, 128), F32),
        in_specs=vmem(1),
        out_specs=vmem(1)[0],
        scratch_shapes=[
            pltpu.VMEM((height_n, slot_rows, 128), F32),
            pltpu.VMEM((devices, slot_rows, 128), BF),
            pltpu.VMEM((devices, slot_rows, 128), BF),
            pltpu.SemaphoreType.DMA((steps,)),
            pltpu.SemaphoreType.DMA((steps,)),
        ],
        compiler_params=pltpu.CompilerParams(
            collective_id=2, has_side_effects=True, vmem_limit_bytes=32 * 2**20
        ),
        name="scatter_grads",
    )(parts)
    summed = summed.reshape(-1)[: 2 * shard].reshape(2, shard)

    new_first = first_decay * first_moment + (1.0 - first_decay) * summed
    new_second = second_decay * second_moment + (1.0 - second_decay) * summed * summed
    first_fix = 1.0 - first_decay**step_count
    second_fix = 1.0 - second_decay**step_count
    new_weights = master_weights - learn_rate * (new_first / first_fix) / (
        jnp.sqrt(new_second / second_fix) + epsilon
    )
    return (features, new_weights, new_first, new_second)


def solution(mesh):
    sizes = (mesh.shape["dp"], mesh.shape["depth"], mesh.shape["height"])
    owners = P(None, ("dp", "depth", "height"))
    blocks = P("dp", "depth", "height", None)
    return jax.shard_map(
        functools.partial(body, sizes),
        mesh=mesh,
        in_specs=(blocks, blocks, owners, owners, owners),
        out_specs=(blocks, owners, owners, owners),
        check_vma=False,
    )
```

```python
import functools

import jax
import jax.numpy as jnp
from jax import lax
from jax.experimental import pallas as pl
from jax.experimental.pallas import tpu as pltpu
from jax.sharding import PartitionSpec as P

C = 64
WIDTH = 64

leak_slope = 0.3
first_decay = 0.9
second_decay = 0.999
learn_rate = 0.001
epsilon = 1e-08
step_count = 10

MESH = pl.DeviceIdType.MESH
BF = jnp.bfloat16
F32 = jnp.float32
SIDES = [(a, b) for a in (-1, 0, 1) for b in (-1, 0, 1) if (a, b) != (0, 0)]


class Groups:
    def __init__(self, sizes):
        dp, depth, height = sizes
        self.line, self.group = height, dp * (depth // 2)
        self.half = self.line * self.group
        p, d, h = lax.axis_index("dp"), lax.axis_index("depth"), lax.axis_index("height")
        pairs = depth // 2
        self.h, self.core = h, lax.rem(d, 2)
        self.q = p * pairs + d // 2
        self.start = self.core * self.half + self.q * self.line
        self.in_line = [
            (lax.rem(h + r, height), lax.rem(h + height - r, height)) for r in range(1, height)
        ]
        self.in_group = [
            (lax.rem(self.q + r, self.group), lax.rem(self.q + self.group - r, self.group))
            for r in range(1, self.group)
        ]
        self.line_ids = [(p, d, to) for to, _ in self.in_line]
        self.group_ids = [
            (to // pairs, 2 * lax.rem(to, pairs) + self.core, h) for to, _ in self.in_group
        ]
        self.core_id = (p, d + 1 - 2 * self.core, h)
        self.ids = self.line_ids + self.group_ids + [self.core_id]
        self.peers = self.line_ids + self.group_ids + [self.core_id] * self.group

    def greet(self):
        barrier = pltpu.get_barrier_semaphore()
        for other in self.ids:
            pl.semaphore_signal(barrier, inc=1, device_id=other, device_id_type=MESH)
        return barrier, len(self.ids)


def gather_kernel(
    sizes,
    own_ref,
    vol_ref,
    all_ref,
    wide_ref,
    vol,
    send_sem,
    recv_sem,
    side_send,
    side_recv,
):
    at = Groups(sizes)
    there, count, id_of = neighbours(sizes[1], sizes[2])
    clear_edges(vol)
    vol[pl.ds(1, vol_ref.shape[0]), pl.ds(1, vol_ref.shape[1])] = vol_ref[...]
    all_ref[pl.ds(at.start + at.h, 1)] = own_ref[...].astype(BF)[None]
    barrier, partners = at.greet()
    signal_neighbours(there, id_of)
    pl.semaphore_wait(barrier, count + partners)
    halo = Halo(vol, there, id_of, side_send, side_recv)

    def copy_of(n, place, size):
        part = all_ref.at[pl.ds(place, size)]
        return pltpu.make_async_remote_copy(
            src_ref=part,
            dst_ref=part,
            send_sem=send_sem.at[n],
            recv_sem=recv_sem.at[n],
            device_id=at.peers[n],
            device_id_type=MESH,
        )

    mine = at.core * at.half
    others = (1 - at.core) * at.half
    line = at.line
    sent = []

    def start(n, place, size):
        sent.append(copy_of(n, place, size))
        sent[-1].start()

    for n in range(len(at.in_line)):
        start(n, at.start + at.h, 1)
    halo.send()
    for n, (_, source) in enumerate(at.in_line):
        copy_of(n, at.start + source, 1).wait_recv()
    first = len(at.in_line)
    core = first + len(at.in_group)
    for n in range(len(at.in_group)):
        start(first + n, at.start, line)
    start(core, at.start, line)
    for n, (_, source) in enumerate(at.in_group):
        copy_of(first + n, mine + source * line, line).wait_recv()
        start(core + 1 + n, mine + source * line, line)
    halo.arrive()
    widen(vol, wide_ref)
    for n, source in enumerate([at.q] + [source for _, source in at.in_group]):
        copy_of(core + n, others + source * line, line).wait_recv()
    for copy in sent:
        copy.wait_send()
    halo.sent()


def scatter_kernel(sizes, grads_ref, out_ref, acc, outgoing, incoming, send_sem, recv_sem):
    at = Groups(sizes)
    barrier, partners = at.greet()
    line, half = at.line, at.half

    def copy_of(n, source, place, size):
        return pltpu.make_async_remote_copy(
            src_ref=outgoing.at[pl.ds(source, size)],
            dst_ref=incoming.at[pl.ds(place, size)],
            send_sem=send_sem.at[n],
            recv_sem=recv_sem.at[n],
            device_id=at.peers[n],
            device_id_type=MESH,
        )

    first = len(at.in_line)
    core = first + len(at.in_group)
    order = [to for to, _ in at.in_group] + [at.q]
    keep, give = at.core * half, (1 - at.core) * half
    pl.semaphore_wait(barrier, partners)
    across = []
    for n, to in enumerate(order):
        there = half + to * line
        outgoing[pl.ds(there, line)] = grads_ref[pl.ds(give + to * line, line)].astype(BF)
        across.append(copy_of(core + n, there, there, line))
        across[-1].start()
    group = []
    for n, to in enumerate(order):
        across[n].wait_recv()
        total = grads_ref[pl.ds(keep + to * line, line)]
        total = total + incoming[pl.ds(half + to * line, line)].astype(F32)
        if n < len(at.in_group):
            outgoing[pl.ds(to * line, line)] = total.astype(BF)
            group.append(copy_of(first + n, to * line, (n + 1) * line, line))
            group[-1].start()
    for n, copy in enumerate(group):
        copy.wait_recv()
        total = total + incoming[pl.ds((n + 1) * line, line)].astype(F32)
    acc[...] = total
    outgoing[pl.ds(at.q * line, line)] = total.astype(BF)
    final = []
    for n, (to, _) in enumerate(at.in_line):
        final.append(copy_of(n, at.q * line + to, n + 1, 1))
        final[-1].start()
    total = acc[pl.ds(at.h, 1)]
    for n, copy in enumerate(final):
        copy.wait_recv()
        total = total + incoming[pl.ds(n + 1, 1)].astype(F32)
    out_ref[...] = total[0]
    for copy in across + group + final:
        copy.wait_send()


def span(side, cells, arriving):
    if side == 0:
        return pl.ds(1, cells)
    if side < 0:
        return pl.ds(cells + 1 if arriving else 1, 1)
    return pl.ds(0 if arriving else cells, 1)


def shifted(x, step, w):
    rolled = pltpu.roll(x, step % x.shape[0], 0)
    edge = 0 if step == 1 else WIDTH - 1
    return jnp.where(w == edge, 0.0, rolled)


def neighbours(depth_n, height_n):
    me_p, me_d, me_h = lax.axis_index("dp"), lax.axis_index("depth"), lax.axis_index("height")

    def there(a, b):
        d, h = me_d + a, me_h + b
        return (d >= 0) & (d < depth_n) & (h >= 0) & (h < height_n)

    near_d = 1 + jnp.where(me_d > 0, 1, 0) + jnp.where(me_d < depth_n - 1, 1, 0)
    near_h = 1 + jnp.where(me_h > 0, 1, 0) + jnp.where(me_h < height_n - 1, 1, 0)
    return there, near_d * near_h - 1, lambda a, b: (me_p, me_d + a, me_h + b)


def signal_neighbours(there, id_of):
    barrier = pltpu.get_barrier_semaphore()
    for a, b in SIDES:

        @pl.when(there(a, b))
        def _(a=a, b=b):
            pl.semaphore_signal(barrier, inc=1, device_id=id_of(a, b), device_id_type=MESH)

    return barrier


def clear_edges(buffer):
    depth, height = buffer.shape[0], buffer.shape[1]
    for d in (0, depth - 1):
        buffer[d] = jnp.zeros_like(buffer[d])
    for h in (0, height - 1):
        buffer[pl.ds(1, depth - 2), h] = jnp.zeros((depth - 2, WIDTH, C), BF)


class Halo:
    def __init__(self, buffer, there, id_of, send_sem, recv_sem):
        self.there, self.copies = there, []
        depth, height = buffer.shape[0] - 2, buffer.shape[1] - 2
        for n, (a, b) in enumerate(SIDES):

            def make(n=n, a=a, b=b):
                return pltpu.make_async_remote_copy(
                    src_ref=buffer.at[span(a, depth, False), span(b, height, False)],
                    dst_ref=buffer.at[span(a, depth, True), span(b, height, True)],
                    send_sem=send_sem.at[n],
                    recv_sem=recv_sem.at[n],
                    device_id=id_of(a, b),
                    device_id_type=MESH,
                )

            self.copies.append(make)

    def each(self, sign, act):
        for make, (a, b) in zip(self.copies, SIDES):

            @pl.when(self.there(sign * a, sign * b))
            def _(make=make):
                act(make())

    def send(self):
        self.each(1, lambda copy: copy.start())

    def arrive(self):
        self.each(-1, lambda copy: copy.wait_recv())

    def sent(self):
        self.each(1, lambda copy: copy.wait_send())


def widen(buffer, wide):
    for b in range(3):
        wide[:, :, :, pl.ds(b * C, C)] = buffer[:, pl.ds(b, wide.shape[1])]


def layers_kernel(
    depth_n,
    height_n,
    slot_of,
    wide_v,
    fg_ref,
    kern_ref,
    feat_ref,
    grad_ref,
    hid,
    del2,
    wide_h,
    slope1,
    slots,
    weights,
    mixed,
    send_sem,
    recv_sem,
):
    cells_d, cells_h = fg_ref.shape[0], fg_ref.shape[1]
    line = cells_h * WIDTH
    there, count, id_of = neighbours(depth_n, height_n)
    if slot_of is not None:
        used = 2 * slot_of[1]
        spare = (grad_ref.shape[0], grad_ref.shape[1] - used, 128)
        grad_ref[:, pl.ds(used, spare[1])] = jnp.zeros(spare, F32)
    clear_edges(hid)
    clear_edges(del2)
    barrier = signal_neighbours(there, id_of)

    half = C // 2
    def assemble(layer):
        for a in range(3):
            for b in range(3):
                taps = [
                    kern_ref[layer, pl.ds((9 * a + 3 * b + c) * half, half)].astype(F32)
                    for c in range(3)
                ]
                for odd in range(2):
                    at = pl.ds(b * C + odd, half, stride=2)
                    parts = [tap[:, odd * C : (odd + 1) * C] for tap in taps]
                    mixed[a, 0, at, :] = jnp.concatenate(parts[:2], 1)
                    mixed[a, 1, at, :] = jnp.concatenate([parts[2], parts[2]], 1)
            weights[layer, a, :, 0 : 2 * C] = mixed[a, 0].astype(BF)
            weights[layer, a, :, 2 * C : 3 * C] = mixed[a, 1, :, 0:C].astype(BF)

    assemble(0)
    pl.semaphore_wait(barrier, count)
    hid_halo = Halo(hid, there, id_of, send_sem.at[0], recv_sem.at[0])
    del_halo = Halo(del2, there, id_of, send_sem.at[1], recv_sem.at[1])

    def width_of(rows):
        return lax.broadcasted_iota(jnp.int32, (rows, C), 0) % WIDTH

    def conv(wide, layer, d):
        total = None
        for a in range(3):
            term = jnp.dot(
                wide[d + a].reshape(line, 3 * C), weights[layer, a], preferred_element_type=F32
            )
            total = term if total is None else total + term
        w = width_of(line)
        return (
            shifted(total[:, 0:C], 1, w)
            + total[:, C : 2 * C]
            + shifted(total[:, 2 * C : 3 * C], -1, w)
        )

    def triple(d, first, layers, delta):
        rows = layers * WIDTH
        w = width_of(rows)
        delta = delta.astype(F32).reshape(rows, C)
        at = pl.ds(first * WIDTH, rows)
        slots[d, at, pl.ds(0, C)] = shifted(delta, -1, w).astype(BF)
        slots[d, at, pl.ds(C, C)] = delta.astype(BF)
        slots[d, at, pl.ds(2 * C, C)] = shifted(delta, 1, w).astype(BF)

    def grad(wide, layer):
        tripled = slots[pl.ds(1, cells_d), pl.ds(WIDTH, line)].reshape(cells_d * line, 3 * C)
        for a in range(3):
            result = lax.dot_general(
                wide[a : a + cells_d].reshape(cells_d * line, 3 * C),
                tripled,
                (((0,), (0,)), ((), ())),
                preferred_element_type=F32,
            )
            mixed[a, 0] = result[:, 0 : 2 * C]
            mixed[a, 1, :, 0:C] = result[:, 2 * C : 3 * C]
            even, odd = (
                [mixed[a, n, pl.ds(first, 3 * half, stride=2), :] for n in range(2)]
                for first in range(2)
            )
            for b in range(3):
                for c in range(3):
                    part = (slice(b * half, (b + 1) * half), slice(c % 2 * C, (c % 2 + 1) * C))
                    tap = jnp.concatenate([even[c // 2][part], odd[c // 2][part]], 1)
                    row = (9 * a + 3 * b + c) * half
                    if slot_of is None:
                        grad_ref[layer, pl.ds(row, half)] = tap
                        continue
                    at, share = 0, slot_of[1]
                    while at < half:
                        owner, skip = divmod(row + at, share)
                        size = min(half - at, share - skip)
                        grad_ref[slot_of[0][owner], pl.ds(layer * share + skip, size)] = tap[
                            at : at + size
                        ]
                        at += size

    for d in range(cells_d):
        linear = conv(wide_v, 0, d)
        slope = jnp.where(linear > 0, 1.0, leak_slope)
        slope1[d] = slope
        hid[d + 1, pl.ds(1, cells_h)] = (linear * slope).astype(BF).reshape(cells_h, WIDTH, C)
    hid_halo.send()
    assemble(1)
    hid_halo.arrive()
    widen(hid, wide_h)
    for d in range(cells_d):
        linear = conv(wide_h, 1, d)
        slope = jnp.where(linear > 0, 1.0, leak_slope)
        feat_ref[d] = (linear * slope).astype(BF).reshape(cells_h, WIDTH, C)
        given = fg_ref[d].astype(F32).reshape(line, C)
        del2[d + 1, pl.ds(1, cells_h)] = (given * slope).astype(BF).reshape(cells_h, WIDTH, C)
    del_halo.send()
    for d in range(1, cells_d + 1):
        triple(d, 1, cells_h, del2[d, pl.ds(1, cells_h)])
    grad(wide_h, 1)
    del_halo.arrive()
    for d in range(cells_d + 2):
        if d in (0, cells_d + 1):
            triple(d, 0, cells_h + 2, del2[d])
        else:
            triple(d, 0, 1, del2[d, 0])
            triple(d, cells_h + 1, 1, del2[d, cells_h + 1])
    deltas = []
    for d in range(cells_d):
        total = None
        for a in range(3):
            spread = lax.dot_general(
                slots[d + 2 - a],
                weights[1, a],
                (((1,), (1,)), ((), ())),
                preferred_element_type=F32,
            )
            for b in range(3):
                term = spread[(2 - b) * WIDTH : (2 - b) * WIDTH + line, b * C : (b + 1) * C]
                total = term if total is None else total + term
        deltas.append((total * slope1[d]).astype(BF))
    for d in range(cells_d):
        triple(d + 1, 1, cells_h, deltas[d])
    grad(wide_v, 0)
    hid_halo.sent()
    del_halo.sent()


def vmem(count):
    return [pl.BlockSpec(memory_space=pltpu.VMEM)] * count


def body(sizes, volume, feature_grad, master_weights, first_moment, second_moment):
    dp_n, depth_n, height_n = sizes
    devices = dp_n * depth_n * height_n
    steps = (height_n - 1) + 2 * dp_n * (depth_n // 2) - 1
    cells_d, cells_h = volume.shape[1], volume.shape[2]
    shard = master_weights.shape[1]
    slot_rows = -(-2 * shard // (16 * 128)) * 16
    pad = slot_rows * 128 - 2 * shard

    slot = jnp.pad(master_weights.reshape(-1), (0, pad)).reshape(slot_rows, 128)
    block = (cells_d, cells_h, WIDTH, C)
    padded = (cells_d + 2, cells_h + 2, WIDTH, C)
    wide = (cells_d + 2, cells_h, WIDTH, 3 * C)
    gathered, wide_volume = pl.pallas_call(
        functools.partial(gather_kernel, sizes),
        out_shape=(
            jax.ShapeDtypeStruct((devices, slot_rows, 128), BF),
            jax.ShapeDtypeStruct(wide, BF),
        ),
        in_specs=vmem(2),
        out_specs=tuple(vmem(2)),
        scratch_shapes=[
            pltpu.VMEM(padded, BF),
            pltpu.SemaphoreType.DMA((steps,)),
            pltpu.SemaphoreType.DMA((steps,)),
            pltpu.SemaphoreType.DMA((8,)),
            pltpu.SemaphoreType.DMA((8,)),
        ],
        compiler_params=pltpu.CompilerParams(
            collective_id=0, has_side_effects=True, vmem_limit_bytes=32 * 2**20
        ),
        name="gather_kernels",
    )(slot, volume.reshape(block))
    if shard % 128 == 0:
        unit = (shard // 128, 128)
        gathered = gathered[:, : 2 * shard // 128]
    else:
        unit = (shard,)
        gathered = gathered.reshape(devices, slot_rows * 128)[:, : 2 * shard]
    order = (4, 1, 2, 0, 3) + tuple(range(5, 5 + len(unit)))
    kernels = (
        gathered.reshape((2, dp_n, depth_n // 2, height_n, 2) + unit)
        .transpose(order)
        .reshape(2, devices * shard // 128, 128)
    )

    slot_of, grads_shape = None, kernels.shape
    if len(unit) == 2 and slot_rows > 2 * unit[0]:
        places = []
        for device in range(devices):
            p, d, h = device // (depth_n * height_n), device // height_n % depth_n, device % height_n
            places.append(((d % 2 * dp_n + p) * (depth_n // 2) + d // 2) * height_n + h)
        slot_of, grads_shape = (places, unit[0]), (devices, slot_rows, 128)

    features, grads = pl.pallas_call(
        functools.partial(layers_kernel, depth_n, height_n, slot_of),
        out_shape=(
            jax.ShapeDtypeStruct(block, BF),
            jax.ShapeDtypeStruct(grads_shape, F32),
        ),
        in_specs=vmem(3),
        out_specs=tuple(vmem(2)),
        scratch_shapes=[
            pltpu.VMEM(padded, BF),
            pltpu.VMEM(padded, BF),
            pltpu.VMEM(wide, BF),
            pltpu.VMEM((cells_d, cells_h * WIDTH, C), F32),
            pltpu.VMEM((cells_d + 2, (cells_h + 2) * WIDTH, 3 * C), BF),
            pltpu.VMEM((2, 3, 3 * C, 3 * C), BF),
            pltpu.VMEM((3, 2, 3 * C, 2 * C), F32),
            pltpu.SemaphoreType.DMA((2, 8)),
            pltpu.SemaphoreType.DMA((2, 8)),
        ],
        compiler_params=pltpu.CompilerParams(
            collective_id=1, has_side_effects=True, vmem_limit_bytes=48 * 2**20
        ),
        name="two_layers",
    )(wide_volume, feature_grad.reshape(block), kernels)
    features = features.reshape(1, cells_d, cells_h, WIDTH * C)

    order = (3, 1, 2, 4, 0) + tuple(range(5, 5 + len(unit)))
    if slot_of is None:
        parts = grads.reshape((2, dp_n, depth_n // 2, 2, height_n) + unit).transpose(order)
    if slot_of is not None:
        parts = grads
    elif len(unit) == 2:
        parts = parts.reshape(devices, 2 * unit[0], 128)
        parts = jnp.pad(parts, ((0, 0), (0, slot_rows - 2 * unit[0]), (0, 0)))
    else:
        parts = jnp.pad(parts.reshape(devices, 2 * shard), ((0, 0), (0, pad)))
        parts = parts.reshape(devices, slot_rows, 128)
    summed = pl.pallas_call(
        functools.partial(scatter_kernel, sizes),
        out_shape=jax.ShapeDtypeStruct((slot_rows, 128), F32),
        in_specs=vmem(1),
        out_specs=vmem(1)[0],
        scratch_shapes=[
            pltpu.VMEM((height_n, slot_rows, 128), F32),
            pltpu.VMEM((devices, slot_rows, 128), BF),
            pltpu.VMEM((devices, slot_rows, 128), BF),
            pltpu.SemaphoreType.DMA((steps,)),
            pltpu.SemaphoreType.DMA((steps,)),
        ],
        compiler_params=pltpu.CompilerParams(
            collective_id=2, has_side_effects=True, vmem_limit_bytes=32 * 2**20
        ),
        name="scatter_grads",
    )(parts)
    summed = summed.reshape(-1)[: 2 * shard].reshape(2, shard)

    new_first = first_decay * first_moment + (1.0 - first_decay) * summed
    new_second = second_decay * second_moment + (1.0 - second_decay) * summed * summed
    first_fix = 1.0 - first_decay**step_count
    second_fix = 1.0 - second_decay**step_count
    new_weights = master_weights - learn_rate * (new_first / first_fix) / (
        jnp.sqrt(new_second / second_fix) + epsilon
    )
    return (features, new_weights, new_first, new_second)


def solution(mesh):
    sizes = (mesh.shape["dp"], mesh.shape["depth"], mesh.shape["height"])
    owners = P(None, ("dp", "depth", "height"))
    blocks = P("dp", "depth", "height", None)
    return jax.shard_map(
        functools.partial(body, sizes),
        mesh=mesh,
        in_specs=(blocks, blocks, owners, owners, owners),
        out_specs=(blocks, owners, owners, owners),
        check_vma=False,
    )
```
